256 devices in a mesh: section: 4 (over y_lo, core), patch: 64 (over y_hi, x, z).
Axes of the slice: x: 4, y: 4 (y_hi: 2, y_lo: 2; y = y_hi * 2 + y_lo), z: 8, core: 2. Of those that a mesh axis runs over, the one named last changes fastest.
Arguments:
- timestep: int32 [1], replicated, may hold values from 0 to 999
- stored: bfloat16 [4, 2, 64, 64, 640], P('section', None, 'patch'), may hold values from -60 to 60
- conv_kernel: bfloat16 [4, 3, 3, 640, 640], P('section'), may hold values from -0.078125 to 0.078125
- conv_bias: float32 [4, 640], P('section'), may hold values from -3 to 3
- group_gain: float32 [4, 640], P('section'), may hold values from 0.1 to 1.9
- group_bias: float32 [4, 640], P('section'), may hold values from -3 to 3
- time_weight: bfloat16 [4, 320, 640], P('section'), may hold values from -0.5 to 0.5
- norm_gain: float32 [4, 640], P('section'), may hold values from 0.1 to 1.9
- norm_bias: float32 [4, 640], P('section'), may hold values from -3 to 3
- w_query: bfloat16 [4, 640, 640], P('section'), may hold values from -7.5104094 to 7.5104094
- w_key: bfloat16 [4, 640, 640], P('section'), may hold values from -0.237170825 to 0.237170825
- w_value: bfloat16 [4, 640, 640], P('section'), may hold values from -0.25 to 0.25
- w_out: bfloat16 [4, 640, 640], P('section'), may hold values from -0.25 to 0.25
Outputs:
- fresh: bfloat16 [4, 2, 64, 64, 640], P('section', None, 'patch')
- handed: bfloat16 [4, 2, 64, 64, 640], P('section', None, 'patch')
The draws below stay inside these ranges and needn't reach their ends.
All inputs are finite; a program needn't handle non-finite values.
Results may differ from the reference program's by a relative error of at most 0.014.
Values may be sent and summed in bfloat16 or wider, within the bound.
A program may use at most 128 MiB of HBM per device.

```python
import jax
import jax.numpy as jnp
from jax import lax

C = 640
TEMB = 320
GROUPS = 32
HEAD_DIM = 64
HEADS = 10
W = 64
H = 64
IMAGES = 2
SECTIONS = 4


def key_base(key):
    values = jax.random.normal(key, (SECTIONS, C, C), jnp.float32)
    return jnp.clip(values, -6.0, 6.0) / jnp.sqrt(jnp.float32(C))


def draw_stored(key, part):
    key = jax.random.fold_in(key, 11)
    proto_key, label_key, noise_key, factor_key = jax.random.split(key, 4)
    labels = jax.random.randint(label_key, (SECTIONS, IMAGES, H * W), 0, 16)
    rows = jnp.arange(H).astype(jnp.float32) / max(H - 1, 1)
    section_ids = jnp.arange(SECTIONS)[:, None, None]
    row_factor = jnp.exp(jax.random.uniform(factor_key, (SECTIONS, IMAGES, H), jnp.float32, -1.2, 1.2))[:, :, :, None, None]
    protos = jnp.clip(jax.random.normal(proto_key, (SECTIONS, 16, C), jnp.float32), -4.0, 4.0)
    noise = jnp.clip(jax.random.normal(noise_key, (SECTIONS, IMAGES, H * W, C), jnp.float32), -4.0, 4.0)
    picked = protos[section_ids, labels]
    values = (0.85 * picked + 0.5 * noise).reshape(SECTIONS, IMAGES, H, W, C)
    growth = (3.0 ** rows)[None, None, :, None, None]
    return (values * growth * row_factor).astype(jnp.bfloat16)


def draw_w_key(key, part):
    base = key_base(key)
    return base.astype(jnp.bfloat16)


def draw_w_query(key, part):
    base = key_base(key)
    key = jax.random.fold_in(key, 23)
    own_key, strength_key = jax.random.split(key)
    own = jnp.clip(jax.random.normal(own_key, (SECTIONS, C, C), jnp.float32), -6.0, 6.0) / jnp.sqrt(jnp.float32(C))
    logs = jax.random.uniform(strength_key, (SECTIONS, 1, HEADS), jnp.float32, jnp.log(0.8), jnp.log(2.0))
    strength = jnp.repeat(jnp.exp(logs), HEAD_DIM, axis=-1)
    return (strength * base + 0.5 * own).astype(jnp.bfloat16)


def steps_of(stream_key, extent, cuts, low, largest):
    def one(axis_at, parts):
        steps = jax.random.uniform(jax.random.fold_in(jax.random.fold_in(stream_key, 6), axis_at), (parts,), jnp.float32, low / len(cuts), largest / len(cuts))
        return jnp.repeat(jnp.exp(steps), extent[axis_at] // parts).reshape((-1,) + (1,) * (len(extent) - axis_at - 1))

    loudness = one(*cuts[0])
    for cut in cuts[1:]:
        loudness = loudness * one(*cut)
    return loudness


def centred(rng, extent, deviation, reach, pieces=(), held_as=jnp.bfloat16):
    loudness = steps_of(rng, extent, pieces, -0.22, 0.18) if pieces else 1.0
    array = jax.random.normal(rng, extent, jnp.float32) * deviation * loudness
    return jnp.minimum(jnp.maximum(array, -reach), reach).astype(held_as)


def setup_inputs(seed: int = 0) -> dict:
    key_list = jax.random.split(jax.random.key(seed), 14)
    return {
        "timestep": jax.random.randint(key_list[0], (1,), 0, 1000).astype(jnp.int32),
        "stored": draw_stored(jax.random.fold_in(key_list[13], 71), 0),
        "conv_kernel": centred(key_list[2], (SECTIONS, 3, 3, C, C), (9 * C) ** -0.5, 0.078125, ((0, 4),)),
        "conv_bias": centred(key_list[3], (SECTIONS, C), 0.5, 3.0, ((0, 4),), jnp.float32),
        "group_gain": jnp.clip(1.0 + 0.18 * jax.random.normal(key_list[4], (SECTIONS, C), jnp.float32), 0.1, 1.9),
        "group_bias": centred(key_list[5], (SECTIONS, C), 0.5, 3.0, ((0, 4),), jnp.float32),
        "time_weight": centred(key_list[6], (SECTIONS, TEMB, C), (TEMB // 2) ** -0.5, 0.5, ((0, 4),)),
        "norm_gain": jnp.clip(1.0 + 0.18 * jax.random.normal(key_list[7], (SECTIONS, C), jnp.float32), 0.1, 1.9),
        "norm_bias": centred(key_list[8], (SECTIONS, C), 0.5, 3.0, ((0, 4),), jnp.float32),
        "w_query": draw_w_query(jax.random.fold_in(key_list[13], 71), 0),
        "w_key": draw_w_key(jax.random.fold_in(key_list[13], 71), 0),
        "w_value": centred(key_list[11], (SECTIONS, C, C), C ** -0.5, 0.25, ((0, 4),)),
        "w_out": centred(key_list[12], (SECTIONS, C, C), C ** -0.5, 0.25, ((0, 4),)),
    }


def time_projection(timestep, weight):
    half = TEMB // 2
    freq = jnp.exp(-jnp.log(10000.0) * jnp.arange(half, dtype=jnp.float32) / half)
    angle = timestep[0].astype(jnp.float32) * freq
    tembed = jnp.concatenate([jnp.cos(angle), jnp.sin(angle)])
    return jnp.dot(jax.nn.silu(tembed)[None, :], weight.astype(jnp.float32), precision=lax.Precision.HIGHEST)[0]

def one_image(x, tproj, kernel, cbias, ggain, gbias, lgain, lbias, wq, wk, wv, wo):
    x32 = x.astype(jnp.float32)
    per = C // GROUPS
    count = float(H * W * per)
    sums = lax.optimization_barrier(jnp.sum(x32, axis=(0, 1))).reshape(GROUPS, per).sum(-1)
    squares = lax.optimization_barrier(jnp.sum(x32 * x32, axis=(0, 1))).reshape(GROUPS, per).sum(-1)
    mean = sums / count
    var = squares / count - mean * mean
    rstd = lax.rsqrt(var + 1e-05)
    scale = jnp.repeat(rstd, per) * ggain
    shift = gbias - jnp.repeat(mean, per) * scale
    activated = jax.nn.silu(x32 * scale + shift).astype(jnp.bfloat16)
    padded = jnp.pad(activated, ((1, 1), (1, 1), (0, 0)))
    taps = [padded[di:di + H, dj:dj + W] for di in range(3) for dj in range(3)]
    patches = jnp.concatenate(taps, axis=-1).reshape(H * W, 9 * C)
    conv = jnp.dot(patches, kernel.reshape(9 * C, C), preferred_element_type=jnp.float32).reshape(H, W, C)
    resid = (x32 + conv + cbias + tproj).astype(jnp.bfloat16)
    r32 = resid.astype(jnp.float32).reshape(H * W, C)
    centre = lax.optimization_barrier(jnp.mean(r32, axis=-1, keepdims=True))
    spread = r32 - centre
    lvar = lax.optimization_barrier(jnp.mean(spread * spread, axis=-1, keepdims=True))
    normed = (spread * lax.rsqrt(lvar + 1e-05) * lgain + lbias).astype(jnp.bfloat16)
    queries = jnp.dot(normed, wq, preferred_element_type=jnp.float32).astype(jnp.bfloat16)
    keys = jnp.dot(normed, wk, preferred_element_type=jnp.float32).astype(jnp.bfloat16)
    values = jnp.dot(normed, wv, preferred_element_type=jnp.float32).astype(jnp.bfloat16)
    qh = queries.astype(jnp.float32).reshape(H * W, HEADS, HEAD_DIM).transpose(1, 0, 2)
    kh = keys.astype(jnp.float32).reshape(H * W, HEADS, HEAD_DIM).transpose(1, 0, 2)
    vh = values.astype(jnp.float32).reshape(H * W, HEADS, HEAD_DIM).transpose(1, 0, 2)

    def one_head(operands):
        qa, ka, va = operands
        score = jnp.dot(qa, ka.T, precision=lax.Precision.HIGHEST) * HEAD_DIM ** (-0.5)
        expo = jnp.exp(score - lax.optimization_barrier(jnp.max(score, axis=-1, keepdims=True)))
        totals = lax.optimization_barrier(jnp.sum(expo, axis=-1, keepdims=True))
        probs = lax.optimization_barrier(expo.astype(jnp.bfloat16)).astype(jnp.float32)
        return jnp.dot(probs, va, precision=lax.Precision.HIGHEST) / totals
    heads_out = lax.map(one_head, (qh, kh, vh))
    attended = heads_out.transpose(1, 0, 2).reshape(H * W, C).astype(jnp.bfloat16)
    mixed = jnp.dot(attended, wo, preferred_element_type=jnp.float32)
    return (r32 + mixed).astype(jnp.bfloat16).reshape(H, W, C)

def component(timestep, x, kernel, cbias, ggain, gbias, tweight, lgain, lbias, wq, wk, wv, wo):
    tproj = time_projection(timestep, tweight)

    def run(image):
        return one_image(image, tproj, kernel, cbias, ggain, gbias, lgain, lbias, wq, wk, wv, wo)
    return lax.map(run, x)

def reference(timestep, stored, conv_kernel, conv_bias, group_gain, group_bias, time_weight, norm_gain, norm_bias, w_query, w_key, w_value, w_out):
    outputs = []
    for section_id in range(SECTIONS):
        outputs.append(component(timestep, stored[section_id], conv_kernel[section_id], conv_bias[section_id], group_gain[section_id], group_bias[section_id], time_weight[section_id], norm_gain[section_id], norm_bias[section_id], w_query[section_id], w_key[section_id], w_value[section_id], w_out[section_id]))
    fresh = jnp.stack(outputs)
    handed = jnp.concatenate([fresh[-1:], fresh[:-1]], axis=0)
    return (fresh, handed)
```

```python
import functools
import math

import jax
import jax.numpy as jnp
from jax import lax
from jax.experimental import pallas as pl
from jax.experimental.pallas import tpu as pltpu
from jax.sharding import PartitionSpec as P

GROUPS = 32
HEAD_DIM = 64
HEADS = 10
C = 640
W = 64
H = 64
IMAGES = 2
TEMB = 320
PER = C // GROUPS
LANES = 128
X = 4
Z = 8
GROUP = 16
KEYS = GROUP * W
QB = 256
F32 = jnp.float32
BF16 = jnp.bfloat16


def thirds(value):
    hi = value.astype(BF16).astype(F32)
    mid = (value - hi).astype(BF16).astype(F32)
    lo = (value - hi - mid).astype(BF16).astype(F32)
    return hi, mid, lo


def exact_dot(value, matrix):
    parts = jnp.concatenate([*thirds(value), jnp.zeros_like(value)], axis=0).astype(BF16)
    out = jnp.dot(parts, matrix, preferred_element_type=F32)
    return out[0:8] + out[8:16] + out[16:24]


def rolled(value):
    return pltpu.roll(value, HEAD_DIM, 1)


def lanes_of(shape):
    return lax.broadcasted_iota(jnp.int32, shape, 1)


def kernel(
    ts_ref, x_hbm, ck_hbm, cb_ref, gg_ref, gb_ref, tw_hbm, ng_ref, nb_ref, wq_hbm, wk_hbm, wv_hbm, wo_hbm,
    fresh_hbm, handed_hbm,
    xin, wc, wt, wq, wk, wv, wo,
    stat_tx, stat_rx, stat2_rx, pad, patches, resid_s,
    send_a, send_b, send_q, recv_a, recv_b, recv_q, kvx, q_main, q_extra,
    m_s, l_s, acc_s, part_tx, part_rx, o_tx, o_rx, att, fresh_s,
    x_sem, w_sem, st_send, st_recv, halo_send, halo_recv,
    a_send, a_recv, b_send, b_recv, q_send, q_recv, f_send, f_recv, qf_send, p_send, p_recv, o_send, o_recv,
    out_sem, h_send, h_recv, loc_sem,
):
    me = lax.axis_index("patch")
    sec = lax.axis_index("section")
    my_y = me // (X * Z)
    my_x = (me // Z) % X
    my_z = me % Z
    my_i = my_y * Z + my_z

    def at(y, x, z):
        return {"patch": y * (X * Z) + x * Z + z}

    def sent(ref, sem):
        pltpu.make_async_copy(ref, ref, sem).wait()

    x_copy = pltpu.make_async_copy(x_hbm.at[0, :, 0], xin.at[1], x_sem)
    x_copy.start()
    loads = [
        pltpu.make_async_copy(tw_hbm.at[0], wt, w_sem.at[0]),
        pltpu.make_async_copy(ck_hbm.at[0], wc, w_sem.at[1]),
        pltpu.make_async_copy(wq_hbm.at[0], wq, w_sem.at[2]),
        pltpu.make_async_copy(wk_hbm.at[0], wk, w_sem.at[3]),
        pltpu.make_async_copy(wv_hbm.at[0], wv, w_sem.at[4]),
        pltpu.make_async_copy(wo_hbm.at[0], wo, w_sem.at[5]),
    ]
    for load in loads:
        load.start()

    barrier = pltpu.get_barrier_semaphore()

    def greet(device):
        pl.semaphore_signal(barrier, inc=1, device_id=device, device_id_type=pl.DeviceIdType.MESH)

    @pl.loop(1, GROUP)
    def _(k):
        i = (my_i + k) % GROUP
        greet(at(i // Z, my_x, i % Z))

    for k in range(1, X):
        greet(at(my_y, (my_x + k) % X, my_z))
    greet({"patch": (me + 1) % H})
    greet({"patch": (me + H - 1) % H})
    greet({"section": (sec + 1) % 4})
    greet({"section": (sec + 3) % 4})

    channel = lax.broadcasted_iota(jnp.int32, (C, LANES), 0)
    group = lax.broadcasted_iota(jnp.int32, (C, LANES), 1)
    gather = ((channel >= group * PER) & (channel < (group + 1) * PER)).astype(F32).astype(BF16)
    group_t = lax.broadcasted_iota(jnp.int32, (LANES, C), 0)
    channel_t = lax.broadcasted_iota(jnp.int32, (LANES, C), 1)
    spread = ((channel_t >= group_t * PER) & (channel_t < (group_t + 1) * PER)).astype(F32).astype(BF16)
    x_copy.wait()
    mine = xin[1].astype(F32)
    sums = [jnp.sum(mine[b], axis=0, keepdims=True) for b in range(IMAGES)]
    squares = [jnp.sum(mine[b] * mine[b], axis=0, keepdims=True) for b in range(IMAGES)]
    stacked = jnp.concatenate([*sums, *squares, jnp.zeros((4, C), F32)], axis=0)
    own_stats = exact_dot(stacked, gather)
    stat_tx[...] = own_stats
    stat_rx[my_i] = own_stats

    pl.semaphore_wait(barrier, GROUP - 1 + X - 1 + 4)

    @pl.loop(1, GROUP)
    def _(k):
        i = (my_i + k) % GROUP
        pltpu.make_async_remote_copy(
            stat_tx, stat_rx.at[my_i], st_send.at[0], st_recv.at[0], device_id=at(i // Z, my_x, i % Z)
        ).start()

    below = pltpu.make_async_remote_copy(
        xin.at[1], xin.at[0], halo_send.at[0], halo_recv.at[0], device_id={"patch": (me + 1) % H}
    )
    above = pltpu.make_async_remote_copy(
        xin.at[1], xin.at[2], halo_send.at[1], halo_recv.at[1], device_id={"patch": (me + H - 1) % H}
    )
    below.start()
    above.start()

    half = TEMB // 2
    place = lax.broadcasted_iota(jnp.int32, (8, TEMB), 1)
    step = jnp.where(place < half, place, place - half).astype(F32)
    angle = ts_ref[0].astype(F32) * jnp.exp(step * (-math.log(10000.0) / half))
    tembed = jnp.where(place < half, jnp.cos(angle), jnp.sin(angle))
    loads[0].wait()
    tproj = exact_dot(tembed * jax.nn.sigmoid(tembed), wt[...])[0:1]
    constant = tproj + cb_ref[...]

    fifteen = stat_rx.at[pl.ds(0, GROUP - 1)]
    sent(fifteen, st_recv.at[0])
    column_stats = jnp.sum(stat_rx[...], axis=0)
    stat2_rx[my_x] = column_stats
    sent(fifteen, st_send.at[0])
    for k in (1, 3, 2):
        pltpu.make_async_remote_copy(
            stat2_rx.at[my_x], stat2_rx.at[my_x], st_send.at[1], st_recv.at[1],
            device_id=at(my_y, (my_x + k) % X, my_z),
        ).start()
    three = stat2_rx.at[pl.ds(0, X - 1)]
    sent(three, st_recv.at[1])
    stats = jnp.sum(stat2_rx[...], axis=0) * (1.0 / (H * W * PER))
    mean = stats[0:2]
    rstd = lax.rsqrt(stats[2:4] - mean * mean + 1e-05)
    wide = exact_dot(jnp.concatenate([mean, rstd, jnp.zeros((4, LANES), F32)], axis=0), spread)
    scale = wide[2:4] * gg_ref[...]
    shift = gb_ref[...] - wide[0:2] * scale

    below.wait_recv()
    above.wait_recv()
    keep = [(me > 0).astype(F32), 1.0, (me < H - 1).astype(F32)]
    edge = jnp.zeros((8, C), F32)
    for b in range(IMAGES):
        for di in range(3):
            line = xin[di, b].astype(F32) * scale[b : b + 1] + shift[b : b + 1]
            line = line * jax.nn.sigmoid(line)
            if di != 1:
                line = line * keep[di]
            pad[b, di, 0:8] = edge
            pad[b, di, 72:80] = edge
            pad[b, di, 8:72] = line
            for dj in range(3):
                tap = di * 3 + dj
                patches[b * W : (b + 1) * W, tap * C : (tap + 1) * C] = pad[b, di, 7 + dj : 71 + dj].astype(BF16)
    loads[1].wait()
    conv = jnp.dot(patches[...], wc[...].reshape(9 * C, C), preferred_element_type=F32)
    resid = (xin[1].astype(F32).reshape(IMAGES * W, C) + conv + constant).astype(BF16)
    resid_s[...] = resid
    r32 = resid.astype(F32)
    centre = jnp.mean(r32, axis=-1, keepdims=True)
    off = r32 - centre
    lvar = jnp.mean(off * off, axis=-1, keepdims=True)
    normed = (off * lax.rsqrt(lvar + 1e-05) * ng_ref[...] + nb_ref[...]).astype(BF16)

    left = lanes_of((W, LANES)) < HEAD_DIM
    left_half = lanes_of((W // 2, LANES)) < HEAD_DIM
    for load in loads[2:5]:
        load.wait()
    queries = jnp.dot(normed, wq[...], preferred_element_type=F32) * (HEAD_DIM**-0.5)
    keys = jnp.dot(normed, wk[...], preferred_element_type=F32)
    values = jnp.dot(normed, wv[...], preferred_element_type=F32)
    for b in range(IMAGES):
        rows = slice(b * W, (b + 1) * W)
        for j in range(HEADS // 2):
            lanes = slice(j * LANES, (j + 1) * LANES)
            k_pair, v_pair, q_pair = keys[rows, lanes], values[rows, lanes], queries[rows, lanes]
            top, bottom = q_pair[: W // 2], q_pair[W // 2 :]
            kv = (jnp.where(left, k_pair, rolled(v_pair)), jnp.where(left, rolled(k_pair), v_pair))
            qq = (jnp.where(left_half, top, rolled(bottom)), jnp.where(left_half, rolled(top), bottom))
            for e in range(2):
                head = 2 * j + e
                if head < Z:
                    send_a[b, head, 0:32] = qq[e].astype(BF16)
                    send_a[b, head, 32:96] = kv[e].astype(BF16)
                else:
                    send_q[b, head - Z] = qq[e].astype(BF16)
                    send_b[b, head - Z] = kv[e].astype(BF16)

    def partner(k):
        m = k // 2
        odd = m % 2
        dz = odd * ((m + 1) // 2) + (1 - odd) * ((Z - m // 2) % Z)
        return (my_y + k % 2) % 2, dz

    @pl.loop(0, GROUP)
    def _(k):
        b, dz = partner(k)
        z = (my_z + dz) % Z

        @pl.when(k == 0)
        def _():
            pltpu.make_async_copy(send_a.at[b, z], recv_a.at[my_i], a_recv.at[my_i]).start()

        @pl.when(k > 0)
        def _():
            pltpu.make_async_remote_copy(
                send_a.at[b, z], recv_a.at[my_i], a_send, a_recv.at[my_i], device_id=at(b, my_x, z)
            ).start()

    member = my_y * 2 + my_z % 2
    for b in range(IMAGES):
        for e in range(2):
            z = my_z // 2 + 4 * e
            here = (z == my_z) & (my_y == b)

            @pl.when(here)
            def _():
                pltpu.make_async_copy(send_q.at[b, e], recv_q.at[my_x, member], q_recv.at[my_x]).start()

            @pl.when(jnp.logical_not(here))
            def _():
                pltpu.make_async_remote_copy(
                    send_q.at[b, e], recv_q.at[my_x, member], q_send.at[b * 2 + e], q_recv.at[my_x],
                    device_id=at(b, my_x, z),
                ).start()

    @pl.loop(0, GROUP)
    def _(k):
        b, dz = partner(k)
        z = (my_z + dz) % Z

        @pl.when(k == 0)
        def _():
            pltpu.make_async_copy(send_b.at[b, z // 4], recv_b.at[my_i], b_recv).start()

        @pl.when(k > 0)
        def _():
            pltpu.make_async_remote_copy(
                send_b.at[b, z // 4], recv_b.at[my_i], b_send, b_recv, device_id=at(b, my_x, z)
            ).start()

    @pl.loop(0, GROUP)
    def _(k):
        y, dz = partner(k)
        z = (my_z + Z - dz) % Z
        i = y * Z + z
        sent(recv_a.at[i], a_recv.at[i])
        chunk = recv_a.at[i, pl.ds(32, W)]
        pltpu.make_async_copy(chunk, kvx.at[my_x, i], f_recv.at[my_x]).start()
        for d in (1, 3, 2):
            pltpu.make_async_remote_copy(
                chunk, kvx.at[my_x, i], f_send, f_recv.at[my_x], device_id=at(my_y, (my_x + d) % X, my_z)
            ).start()

    sent(recv_q.at[my_x], q_recv.at[my_x])
    for d in (1, 3, 2):
        pltpu.make_async_remote_copy(
            recv_q.at[my_x], recv_q.at[my_x], qf_send, q_recv.at[my_x],
            device_id=at(my_y, (my_x + d) % X, my_z),
        ).start()

    def unpack(packed, out, base):
        wide = packed.astype(F32)
        out[pl.ds(base, 32)] = jnp.where(left_half, wide, 0.0).astype(BF16)
        out[pl.ds(base + 32, 32)] = jnp.where(left_half, rolled(wide), 0.0).astype(BF16)

    @pl.loop(0, GROUP)
    def _(i):
        unpack(recv_a[i, 0:32], q_main, pl.multiple_of(i * W, W))

    def block(q, kv, carry):
        score = lax.dot_general(q, kv, (((1,), (1,)), ((), ())), preferred_element_type=F32)
        top = jnp.max(score, axis=-1, keepdims=True)
        if carry is not None:
            top = jnp.maximum(carry[0], top)
        expo = jnp.exp(score - top)
        total = jnp.sum(expo, axis=-1, keepdims=True)
        out = jnp.dot(expo.astype(BF16), kv, preferred_element_type=F32)
        if carry is not None:
            fade = jnp.exp(carry[0] - top)
            total = total + fade * carry[1]
            out = out + fade * carry[2]
        return top, total, out

    def column(t):
        return (my_x + (t + t // 2 - 2 * (t // 3))) % X

    def keys_of(c):
        return kvx[c].reshape(KEYS, LANES)

    def main_step(c, first):
        sent(kvx.at[c], f_recv.at[c])

        @pl.loop(0, KEYS // QB)
        def _(n):
            rows = pl.ds(pl.multiple_of(n * QB, QB), QB)
            carry = None if first else (m_s[rows], l_s[rows], acc_s[rows])
            top, total, out = block(q_main[rows], keys_of(c), carry)
            m_s[rows] = top
            l_s[rows] = total
            acc_s[rows] = out

    main_step(my_x, True)
    main_step((my_x + 1) % X, False)

    for d in (1, 3, 2):
        c = (my_x + d) % X
        sent(recv_q.at[c], q_recv.at[c])
    sent(recv_b, b_recv)

    @pl.loop(0, GROUP)
    def _(i):
        unpack(recv_q[i // 4, i % 4], q_extra, pl.multiple_of(i * W, W))

    lanes_q = lanes_of((QB, LANES))

    @pl.loop(0, X)
    def _(t):
        c = (my_x + t + 1) % X
        rows = pl.ds(pl.multiple_of(c * QB, QB), QB)
        top, total, out = block(q_extra[rows], recv_b[...].reshape(KEYS, LANES), None)
        hi, mid, lo = thirds(top + jnp.log(total))
        lse = jnp.where(lanes_q < 16, hi, jnp.where(lanes_q < 32, mid, lo))
        packed = jnp.where(lanes_q < HEAD_DIM, lse, out / total).astype(BF16)

        @pl.when(t < X - 1)
        def _():
            part_tx[t] = packed
            pltpu.make_async_remote_copy(
                part_tx.at[t], part_rx.at[my_x], p_send.at[t], p_recv, device_id=at(my_y, c, my_z)
            ).start()

        @pl.when(t == X - 1)
        def _():
            part_rx[my_x] = packed

    main_step((my_x + 3) % X, False)

    def pack_rows(out, r):
        top, bottom = out[r * W : r * W + 32], out[r * W + 32 : (r + 1) * W]
        return jnp.where(left_half, rolled(top), bottom).astype(BF16)

    def home(slot, i, head):
        y, z = i // Z, i % Z

        @pl.when(i == my_i)
        def _():
            pltpu.make_async_copy(o_tx.at[slot], o_rx.at[my_y, head], o_recv).start()

        @pl.when(i != my_i)
        def _():
            pltpu.make_async_remote_copy(
                o_tx.at[slot], o_rx.at[my_y, head], o_send, o_recv, device_id=at(y, my_x, z)
            ).start()

    last = (my_x + 2) % X
    sent(kvx.at[last], f_recv.at[last])

    @pl.loop(0, KEYS // QB)
    def _(n):
        rows = pl.ds(pl.multiple_of(n * QB, QB), QB)
        top, total, out = block(q_main[rows], keys_of(last), (m_s[rows], l_s[rows], acc_s[rows]))
        out = out / total
        for r in range(QB // W):
            o_tx[n * (QB // W) + r] = pack_rows(out, r)
        for r in range(QB // W):
            home(n * (QB // W) + r, n * (QB // W) + r, my_z)

    sent(part_rx.at[pl.ds(0, X - 1)], p_recv)
    parts = [part_rx[c].astype(F32) for c in range(X)]
    lses = [p[:, 0:1] + p[:, 16:17] + p[:, 32:33] for p in parts]
    peak = functools.reduce(jnp.maximum, lses)
    weights = [jnp.exp(lse - peak) for lse in lses]
    merged = sum(w * p for w, p in zip(weights, parts)) / sum(weights)
    for r in range(4):
        o_tx[GROUP + r] = pack_rows(merged, r)
    for r in range(4):
        quarter = my_z % 4
        home(GROUP + r, (r // 2) * Z + quarter * 2 + r % 2, Z + my_z // 4)

    sent(o_rx, o_recv)
    for b in range(IMAGES):
        for j in range(HEADS // 2):
            even, odd = o_rx[b, 2 * j].astype(F32), o_rx[b, 2 * j + 1].astype(F32)
            att[b * W : b * W + 32, j * LANES : (j + 1) * LANES] = jnp.where(left_half, even, rolled(odd)).astype(BF16)
            att[b * W + 32 : (b + 1) * W, j * LANES : (j + 1) * LANES] = jnp.where(
                left_half, rolled(even), odd
            ).astype(BF16)
    loads[5].wait()
    mixed = jnp.dot(att[...], wo[...], preferred_element_type=F32)
    fresh_s[...] = (resid_s[...].astype(F32) + mixed).astype(BF16).reshape(IMAGES, W, C)
    pass_on = pltpu.make_async_remote_copy(
        fresh_s, handed_hbm.at[0, :, 0], h_send, h_recv, device_id={"section": (sec + 1) % 4}
    )
    pass_on.start()
    keep_copy = pltpu.make_async_copy(fresh_s, fresh_hbm.at[0, :, 0], out_sem)
    keep_copy.start()

    below.wait_send()
    above.wait_send()
    sent(three, st_send.at[1])
    sent(recv_a.at[pl.ds(0, GROUP - 1)], a_send)
    sent(recv_b.at[pl.ds(0, GROUP - 1)], b_send)
    for b in range(IMAGES):
        for e in range(2):
            here = (my_z // 2 + 4 * e == my_z) & (my_y == b)

            @pl.when(jnp.logical_not(here))
            def _():
                sent(send_q.at[b, e], q_send.at[b * 2 + e])

    sent(kvx.at[pl.ds(0, X - 1)], f_send)
    sent(recv_q.at[pl.ds(0, X - 1)], qf_send)
    for t in range(X - 1):
        sent(part_tx.at[t], p_send.at[t])
    at_home = (my_z % 4) == (my_z // 2)

    @pl.when(at_home)
    def _():
        sent(o_tx.at[pl.ds(0, GROUP + 4 - 2)], o_send)

    @pl.when(jnp.logical_not(at_home))
    def _():
        sent(o_tx.at[pl.ds(0, GROUP + 4 - 1)], o_send)

    keep_copy.wait()
    pass_on.wait()


def body(*args):
    any_space = pl.BlockSpec(memory_space=pl.ANY)
    vmem = pl.BlockSpec(memory_space=pltpu.VMEM)
    out = jax.ShapeDtypeStruct((1, IMAGES, 1, W, C), BF16)
    dma = pltpu.SemaphoreType.DMA
    return pl.pallas_call(
        kernel,
        out_shape=(out, out),
        in_specs=[
            pl.BlockSpec(memory_space=pltpu.SMEM), any_space, any_space, vmem, vmem, vmem, any_space, vmem, vmem,
            any_space, any_space, any_space, any_space,
        ],
        out_specs=(any_space, any_space),
        scratch_shapes=[
            pltpu.VMEM((3, IMAGES, W, C), BF16),
            pltpu.VMEM((3, 3, C, C), BF16),
            pltpu.VMEM((TEMB, C), BF16),
            pltpu.VMEM((C, C), BF16),
            pltpu.VMEM((C, C), BF16),
            pltpu.VMEM((C, C), BF16),
            pltpu.VMEM((C, C), BF16),
            pltpu.VMEM((8, LANES), F32),
            pltpu.VMEM((GROUP, 8, LANES), F32),
            pltpu.VMEM((X, 8, LANES), F32),
            pltpu.VMEM((IMAGES, 3, W + 16, C), F32),
            pltpu.VMEM((IMAGES * W, 9 * C), BF16),
            pltpu.VMEM((IMAGES * W, C), BF16),
            pltpu.VMEM((IMAGES, Z, 96, LANES), BF16),
            pltpu.VMEM((IMAGES, 2, W, LANES), BF16),
            pltpu.VMEM((IMAGES, 2, W // 2, LANES), BF16),
            pltpu.VMEM((GROUP, 96, LANES), BF16),
            pltpu.VMEM((GROUP, W, LANES), BF16),
            pltpu.VMEM((X, 4, W // 2, LANES), BF16),
            pltpu.VMEM((X, GROUP, W, LANES), BF16),
            pltpu.VMEM((KEYS, LANES), BF16),
            pltpu.VMEM((KEYS, LANES), BF16),
            pltpu.VMEM((KEYS, 1), F32),
            pltpu.VMEM((KEYS, 1), F32),
            pltpu.VMEM((KEYS, LANES), F32),
            pltpu.VMEM((X - 1, QB, LANES), BF16),
            pltpu.VMEM((X, QB, LANES), BF16),
            pltpu.VMEM((GROUP + 4, W // 2, LANES), BF16),
            pltpu.VMEM((IMAGES, HEADS, W // 2, LANES), BF16),
            pltpu.VMEM((IMAGES * W, C), BF16),
            pltpu.VMEM((IMAGES, W, C), BF16),
            dma,
            dma((6,)),
            dma((2,)),
            dma((2,)),
            dma((2,)),
            dma((2,)),
            dma,
            dma((GROUP,)),
            dma,
            dma,
            dma((4,)),
            dma((X,)),
            dma,
            dma((X,)),
            dma,
            dma((X - 1,)),
            dma,
            dma,
            dma,
            dma,
            dma,
            dma,
            dma,
        ],
        compiler_params=pltpu.CompilerParams(
            collective_id=0, has_side_effects=True, vmem_limit_bytes=48 * 1024 * 1024
        ),
    )(*args)


def solution(mesh):
    placed = (
        P(),
        P("section", None, "patch", None, None),
        P("section", None, None, None, None),
        P("section", None),
        P("section", None),
        P("section", None),
        P("section", None, None),
        P("section", None),
        P("section", None),
        P("section", None, None),
        P("section", None, None),
        P("section", None, None),
        P("section", None, None),
    )
    whole = P("section", None, "patch", None, None)
    return jax.shard_map(body, mesh=mesh, in_specs=placed, out_specs=(whole, whole), check_vma=False)
```

```python
import functools
import math

import jax
import jax.numpy as jnp
from jax import lax
from jax.experimental import pallas as pl
from jax.experimental.pallas import tpu as pltpu
from jax.sharding import PartitionSpec as P

GROUPS = 32
HEAD_DIM = 64
HEADS = 10
C = 640
W = 64
H = 64
IMAGES = 2
TEMB = 320
PER = C // GROUPS
LANES = 128
X = 4
Z = 8
GROUP = 16
KEYS = GROUP * W
QB = 256
F32 = jnp.float32
BF16 = jnp.bfloat16


def thirds(value):
    hi = value.astype(BF16).astype(F32)
    mid = (value - hi).astype(BF16).astype(F32)
    lo = (value - hi - mid).astype(BF16).astype(F32)
    return hi, mid, lo


def exact_dot(value, matrix):
    parts = jnp.concatenate([*thirds(value), jnp.zeros_like(value)], axis=0).astype(BF16)
    out = jnp.dot(parts, matrix, preferred_element_type=F32)
    return out[0:8] + out[8:16] + out[16:24]


def rolled(value):
    return pltpu.roll(value, HEAD_DIM, 1)


def lanes_of(shape):
    return lax.broadcasted_iota(jnp.int32, shape, 1)


def kernel(
    ts_hbm, x_hbm, ck_hbm, cb_hbm, gg_hbm, gb_hbm, tw_hbm, ng_hbm, nb_hbm, wq_hbm, wk_hbm, wv_hbm, wo_hbm,
    fresh_hbm, handed_hbm,
    ts_ref, vectors, xin, wc, wt, wq, wk, wv, wo,
    stat_tx, stat_rx, stat2_rx, pad, patches, resid_s,
    send_a, send_b, send_q, recv_a, recv_b, recv_q, kvx, q_main, q_extra,
    m_s, acc_s, part_tx, part_rx, o_tx, o_rx, att, fresh_s,
    x_sem, w_sem, st_send, st_recv, halo_send, halo_recv,
    a_send, a_recv, b_send, b_recv, q_send, q_recv, f_send, f_recv, qf_send, p_send, p_recv, o_send, o_recv,
    out_sem, h_send, h_recv, v_sem,
):
    me = lax.axis_index("patch")
    sec = lax.axis_index("section")
    my_y = me // (X * Z)
    my_x = (me // Z) % X
    my_z = me % Z
    my_i = my_y * Z + my_z

    def at(y, x, z):
        return {"patch": y * (X * Z) + x * Z + z}

    def sent(ref, sem):
        pltpu.make_async_copy(ref, ref, sem).wait()

    x_copy = pltpu.make_async_copy(x_hbm.at[0, :, 0], xin.at[1], x_sem)
    x_copy.start()
    loads = [
        pltpu.make_async_copy(tw_hbm.at[0], wt, w_sem.at[0]),
        pltpu.make_async_copy(ck_hbm.at[0], wc, w_sem.at[1]),
        pltpu.make_async_copy(wq_hbm.at[0], wq, w_sem.at[2]),
        pltpu.make_async_copy(wk_hbm.at[0], wk, w_sem.at[3]),
        pltpu.make_async_copy(wv_hbm.at[0], wv, w_sem.at[4]),
        pltpu.make_async_copy(wo_hbm.at[0], wo, w_sem.at[5]),
    ]
    small = [
        pltpu.make_async_copy(ref, vectors.at[n], v_sem.at[n])
        for n, ref in enumerate((cb_hbm, gg_hbm, gb_hbm, ng_hbm, nb_hbm))
    ]
    small.append(pltpu.make_async_copy(ts_hbm, ts_ref, v_sem.at[5]))
    for load in [*small, *loads]:
        load.start()

    barrier = pltpu.get_barrier_semaphore()

    def greet(device):
        pl.semaphore_signal(barrier, inc=1, device_id=device, device_id_type=pl.DeviceIdType.MESH)

    @pl.loop(1, GROUP)
    def _(k):
        i = (my_i + k) % GROUP
        greet(at(i // Z, my_x, i % Z))

    for k in range(1, X):
        greet(at(my_y, (my_x + k) % X, my_z))
    greet({"patch": (me + 1) % H})
    greet({"patch": (me + H - 1) % H})
    greet({"section": (sec + 1) % 4})
    greet({"section": (sec + 3) % 4})

    channel = lax.broadcasted_iota(jnp.int32, (C, LANES), 0)
    group = lax.broadcasted_iota(jnp.int32, (C, LANES), 1)
    gather = ((channel >= group * PER) & (channel < (group + 1) * PER)).astype(F32).astype(BF16)
    group_t = lax.broadcasted_iota(jnp.int32, (LANES, C), 0)
    channel_t = lax.broadcasted_iota(jnp.int32, (LANES, C), 1)
    spread = ((channel_t >= group_t * PER) & (channel_t < (group_t + 1) * PER)).astype(F32).astype(BF16)
    x_copy.wait()
    mine = xin[1].astype(F32)
    sums = [jnp.sum(mine[b], axis=0, keepdims=True) for b in range(IMAGES)]
    squares = [jnp.sum(mine[b] * mine[b], axis=0, keepdims=True) for b in range(IMAGES)]
    stacked = jnp.concatenate([*sums, *squares, jnp.zeros((4, C), F32)], axis=0)
    own_stats = exact_dot(stacked, gather)
    stat_tx[...] = own_stats
    stat_rx[my_i] = own_stats

    pl.semaphore_wait(barrier, GROUP - 1 + X - 1 + 4)

    @pl.loop(1, GROUP)
    def _(k):
        i = (my_i + k) % GROUP
        pltpu.make_async_remote_copy(
            stat_tx, stat_rx.at[my_i], st_send.at[0], st_recv.at[0], device_id=at(i // Z, my_x, i % Z)
        ).start()

    below = pltpu.make_async_remote_copy(
        xin.at[1], xin.at[0], halo_send.at[0], halo_recv.at[0], device_id={"patch": (me + 1) % H}
    )
    above = pltpu.make_async_remote_copy(
        xin.at[1], xin.at[2], halo_send.at[1], halo_recv.at[1], device_id={"patch": (me + H - 1) % H}
    )
    below.start()
    above.start()

    half = TEMB // 2
    place = lax.broadcasted_iota(jnp.int32, (8, TEMB), 1)
    step = jnp.where(place < half, place, place - half).astype(F32)
    for load in small:
        load.wait()
    angle = ts_ref[0].astype(F32) * jnp.exp(step * (-math.log(10000.0) / half))
    tembed = jnp.where(place < half, jnp.cos(angle), jnp.sin(angle))
    loads[0].wait()
    tproj = exact_dot(tembed * jax.nn.sigmoid(tembed), wt[...])[0:1]
    constant = tproj + vectors[0]

    fifteen = stat_rx.at[pl.ds(0, GROUP - 1)]
    sent(fifteen, st_recv.at[0])
    column_stats = jnp.sum(stat_rx[...], axis=0)
    stat2_rx[my_x] = column_stats
    sent(fifteen, st_send.at[0])
    for k in (1, 3, 2):
        pltpu.make_async_remote_copy(
            stat2_rx.at[my_x], stat2_rx.at[my_x], st_send.at[1], st_recv.at[1],
            device_id=at(my_y, (my_x + k) % X, my_z),
        ).start()
    three = stat2_rx.at[pl.ds(0, X - 1)]
    sent(three, st_recv.at[1])
    stats = jnp.sum(stat2_rx[...], axis=0) * (1.0 / (H * W * PER))
    mean = stats[0:2]
    rstd = lax.rsqrt(stats[2:4] - mean * mean + 1e-05)
    wide = exact_dot(jnp.concatenate([mean, rstd, jnp.zeros((4, LANES), F32)], axis=0), spread)
    scale = wide[2:4] * vectors[1]
    shift = vectors[2] - wide[0:2] * scale

    below.wait_recv()
    above.wait_recv()
    keep = [(me > 0).astype(F32), 1.0, (me < H - 1).astype(F32)]
    edge = jnp.zeros((8, C), F32)
    for b in range(IMAGES):
        for di in range(3):
            line = xin[di, b].astype(F32) * scale[b : b + 1] + shift[b : b + 1]
            line = line * jax.nn.sigmoid(line)
            if di != 1:
                line = line * keep[di]
            pad[b, di, 0:8] = edge
            pad[b, di, 72:80] = edge
            pad[b, di, 8:72] = line
            for dj in range(3):
                tap = di * 3 + dj
                patches[b * W : (b + 1) * W, tap * C : (tap + 1) * C] = pad[b, di, 7 + dj : 71 + dj].astype(BF16)
    loads[1].wait()
    conv = jnp.dot(patches[...], wc[...].reshape(9 * C, C), preferred_element_type=F32)
    resid = (xin[1].astype(F32).reshape(IMAGES * W, C) + conv + constant).astype(BF16)
    resid_s[...] = resid
    r32 = resid.astype(F32)
    centre = jnp.mean(r32, axis=-1, keepdims=True)
    off = r32 - centre
    lvar = jnp.mean(off * off, axis=-1, keepdims=True)
    normed = (off * lax.rsqrt(lvar + 1e-05) * vectors[3] + vectors[4]).astype(BF16)

    left = lanes_of((W, LANES)) < HEAD_DIM
    left_half = lanes_of((W // 2, LANES)) < HEAD_DIM
    for load in loads[2:5]:
        load.wait()
    queries = jnp.dot(normed, wq[...], preferred_element_type=F32) * (HEAD_DIM**-0.5)
    keys = jnp.dot(normed, wk[...], preferred_element_type=F32)
    values = jnp.dot(normed, wv[...], preferred_element_type=F32)
    for b in range(IMAGES):
        rows = slice(b * W, (b + 1) * W)
        for j in range(HEADS // 2):
            lanes = slice(j * LANES, (j + 1) * LANES)
            k_pair, v_pair, q_pair = keys[rows, lanes], values[rows, lanes], queries[rows, lanes]
            top, bottom = q_pair[: W // 2], q_pair[W // 2 :]
            kv = (jnp.where(left, k_pair, rolled(v_pair)), jnp.where(left, rolled(k_pair), v_pair))
            qq = (jnp.where(left_half, top, rolled(bottom)), jnp.where(left_half, rolled(top), bottom))
            for e in range(2):
                head = 2 * j + e
                if head < Z:
                    send_a[b, head, 0:32] = qq[e].astype(BF16)
                    send_a[b, head, 32:96] = kv[e].astype(BF16)
                else:
                    send_q[b, head - Z] = qq[e].astype(BF16)
                    send_b[b, head - Z] = kv[e].astype(BF16)

    def partner(k):
        m = k // 2
        odd = m % 2
        dz = odd * ((m + 1) // 2) + (1 - odd) * ((Z - m // 2) % Z)
        return (my_y + k % 2) % 2, dz

    @pl.loop(0, GROUP)
    def _(k):
        b, dz = partner(k)
        z = (my_z + dz) % Z

        @pl.when(k == 0)
        def _():
            pltpu.make_async_copy(send_a.at[b, z], recv_a.at[my_i], a_recv.at[my_i]).start()

        @pl.when(k > 0)
        def _():
            pltpu.make_async_remote_copy(
                send_a.at[b, z], recv_a.at[my_i], a_send, a_recv.at[my_i], device_id=at(b, my_x, z)
            ).start()

    member = my_y * 2 + my_z % 2
    for b in range(IMAGES):
        for e in range(2):
            z = my_z // 2 + 4 * e
            here = (z == my_z) & (my_y == b)

            @pl.when(here)
            def _():
                pltpu.make_async_copy(send_q.at[b, e], recv_q.at[my_x, member], q_recv.at[my_x]).start()

            @pl.when(jnp.logical_not(here))
            def _():
                pltpu.make_async_remote_copy(
                    send_q.at[b, e], recv_q.at[my_x, member], q_send.at[b * 2 + e], q_recv.at[my_x],
                    device_id=at(b, my_x, z),
                ).start()

    @pl.loop(0, GROUP)
    def _(k):
        b, dz = partner(k)
        z = (my_z + dz) % Z

        @pl.when(k == 0)
        def _():
            pltpu.make_async_copy(send_b.at[b, z // 4], recv_b.at[my_i], b_recv).start()

        @pl.when(k > 0)
        def _():
            pltpu.make_async_remote_copy(
                send_b.at[b, z // 4], recv_b.at[my_i], b_send, b_recv, device_id=at(b, my_x, z)
            ).start()

    @pl.loop(0, GROUP)
    def _(k):
        y, dz = partner(k)
        z = (my_z + Z - dz) % Z
        i = y * Z + z
        sent(recv_a.at[i], a_recv.at[i])
        chunk = recv_a.at[i, pl.ds(32, W)]
        pltpu.make_async_copy(chunk, kvx.at[my_x, i], f_recv.at[my_x]).start()
        for d in (1, 3, 2):
            pltpu.make_async_remote_copy(
                chunk, kvx.at[my_x, i], f_send, f_recv.at[my_x], device_id=at(my_y, (my_x + d) % X, my_z)
            ).start()

    sent(recv_q.at[my_x], q_recv.at[my_x])
    for d in (1, 3, 2):
        pltpu.make_async_remote_copy(
            recv_q.at[my_x], recv_q.at[my_x], qf_send, q_recv.at[my_x],
            device_id=at(my_y, (my_x + d) % X, my_z),
        ).start()

    def unpack(packed, out, base):
        wide = packed.astype(F32)
        out[pl.ds(base, 32)] = jnp.where(left_half, wide, 0.0).astype(BF16)
        out[pl.ds(base + 32, 32)] = jnp.where(left_half, rolled(wide), 0.0).astype(BF16)

    @pl.loop(0, GROUP)
    def _(i):
        unpack(recv_a[i, 0:32], q_main, pl.multiple_of(i * W, W))

    def rows_of(n):
        return slice(n * QB, (n + 1) * QB)

    lane_k = lanes_of((KEYS, LANES))

    def score_of(q, kv):
        return lax.dot_general(q, kv, (((1,), (1,)), ((), ())), preferred_element_type=F32)

    def softened(score, old):
        pieces = [score[:, i * LANES : (i + 1) * LANES] for i in range(KEYS // LANES)]
        top = jnp.max(functools.reduce(jnp.maximum, pieces), axis=-1, keepdims=True)
        top = jnp.broadcast_to(top, (QB, LANES))
        if old is not None:
            top = jnp.maximum(old, top)
        probs = jnp.concatenate([jnp.exp(piece - top).astype(BF16) for piece in pieces], axis=1)
        return top, probs, None if old is None else jnp.exp(old - top)

    def attend(kv, queries, old_tops, old_sums, done):
        ones_values = jnp.where(lane_k < HEAD_DIM, 1.0, kv.astype(F32)).astype(BF16)
        blocks = KEYS // QB
        score = score_of(queries(0), kv)
        for n in range(blocks):
            following = score_of(queries(n + 1), kv) if n + 1 < blocks else None
            top, probs, fade = softened(score, None if old_tops is None else old_tops(n))
            out = jnp.dot(probs, ones_values, preferred_element_type=F32)
            if fade is not None:
                out = out + fade * old_sums(n)
            done(n, top, out)
            score = following

    def keys_of(c):
        return kvx[c].reshape(KEYS, LANES)

    def main_queries(n):
        return q_main[rows_of(n)]

    def main_tops(n):
        return m_s[rows_of(n)]

    def main_sums(n):
        return acc_s[rows_of(n)]

    def keep_main(n, top, out):
        m_s[rows_of(n)] = top
        acc_s[rows_of(n)] = out

    sent(kvx.at[my_x], f_recv.at[my_x])
    attend(keys_of(my_x), main_queries, None, None, keep_main)

    def main_step(d):
        c = (my_x + d) % X
        sent(kvx.at[c], f_recv.at[c])
        attend(keys_of(c), main_queries, main_tops, main_sums, keep_main)

    main_step(1)

    for d in (1, 3, 2):
        c = (my_x + d) % X
        sent(recv_q.at[c], q_recv.at[c])
    sent(recv_b, b_recv)

    @pl.loop(0, GROUP)
    def _(i):
        unpack(recv_q[i // 4, i % 4], q_extra, pl.multiple_of(i * W, W))

    lanes_q = lanes_of((QB, LANES))

    def extra_queries(n):
        c = (my_x + n + 1) % X
        return q_extra[pl.ds(pl.multiple_of(c * QB, QB), QB)]

    def extra_done(n, top, out):
        total = out[:, 0:1]
        hi, mid, lo = thirds(top + jnp.log(total))
        lse = jnp.where(lanes_q < 16, hi, jnp.where(lanes_q < 32, mid, lo))
        packed = jnp.where(lanes_q < HEAD_DIM, lse, out / total).astype(BF16)
        if n < X - 1:
            part_tx[n] = packed
            pltpu.make_async_remote_copy(
                part_tx.at[n], part_rx.at[my_x], p_send.at[n], p_recv, device_id=at(my_y, (my_x + n + 1) % X, my_z)
            ).start()
        else:
            part_rx[my_x] = packed

    attend(recv_b[...].reshape(KEYS, LANES), extra_queries, None, None, extra_done)
    main_step(3)

    def pack_rows(out, r):
        top, bottom = out[r * W : r * W + 32], out[r * W + 32 : (r + 1) * W]
        return jnp.where(left_half, rolled(top), bottom).astype(BF16)

    def home(slot, i, head):
        y, z = i // Z, i % Z

        @pl.when(i == my_i)
        def _():
            pltpu.make_async_copy(o_tx.at[slot], o_rx.at[my_y, head], o_recv).start()

        @pl.when(i != my_i)
        def _():
            pltpu.make_async_remote_copy(
                o_tx.at[slot], o_rx.at[my_y, head], o_send, o_recv, device_id=at(y, my_x, z)
            ).start()

    last = (my_x + 2) % X
    sent(kvx.at[last], f_recv.at[last])

    def main_done(n, top, out):
        out = out / out[:, 0:1]
        for r in range(QB // W):
            o_tx[n * (QB // W) + r] = pack_rows(out, r)
        for r in range(QB // W):
            home(n * (QB // W) + r, n * (QB // W) + r, my_z)

    attend(keys_of(last), main_queries, main_tops, main_sums, main_done)

    sent(part_rx.at[pl.ds(0, X - 1)], p_recv)
    parts = [part_rx[c].astype(F32) for c in range(X)]
    lses = [p[:, 0:1] + p[:, 16:17] + p[:, 32:33] for p in parts]
    peak = functools.reduce(jnp.maximum, lses)
    weights = [jnp.exp(lse - peak) for lse in lses]
    merged = sum(w * p for w, p in zip(weights, parts)) / sum(weights)
    for r in range(4):
        o_tx[GROUP + r] = pack_rows(merged, r)
    for r in range(4):
        quarter = my_z % 4
        home(GROUP + r, (r // 2) * Z + quarter * 2 + r % 2, Z + my_z // 4)

    sent(o_rx, o_recv)
    for b in range(IMAGES):
        for j in range(HEADS // 2):
            even, odd = o_rx[b, 2 * j].astype(F32), o_rx[b, 2 * j + 1].astype(F32)
            att[b * W : b * W + 32, j * LANES : (j + 1) * LANES] = jnp.where(left_half, even, rolled(odd)).astype(BF16)
            att[b * W + 32 : (b + 1) * W, j * LANES : (j + 1) * LANES] = jnp.where(
                left_half, rolled(even), odd
            ).astype(BF16)
    loads[5].wait()
    mixed = jnp.dot(att[...], wo[...], preferred_element_type=F32)
    fresh_s[...] = (resid_s[...].astype(F32) + mixed).astype(BF16).reshape(IMAGES, W, C)
    pass_on = pltpu.make_async_remote_copy(
        fresh_s, handed_hbm.at[0, :, 0], h_send, h_recv, device_id={"section": (sec + 1) % 4}
    )
    pass_on.start()
    keep_copy = pltpu.make_async_copy(fresh_s, fresh_hbm.at[0, :, 0], out_sem)
    keep_copy.start()

    below.wait_send()
    above.wait_send()
    sent(three, st_send.at[1])
    sent(recv_a.at[pl.ds(0, GROUP - 1)], a_send)
    sent(recv_b.at[pl.ds(0, GROUP - 1)], b_send)
    for b in range(IMAGES):
        for e in range(2):
            here = (my_z // 2 + 4 * e == my_z) & (my_y == b)

            @pl.when(jnp.logical_not(here))
            def _():
                sent(send_q.at[b, e], q_send.at[b * 2 + e])

    sent(kvx.at[pl.ds(0, X - 1)], f_send)
    sent(recv_q.at[pl.ds(0, X - 1)], qf_send)
    for t in range(X - 1):
        sent(part_tx.at[t], p_send.at[t])
    at_home = (my_z % 4) == (my_z // 2)

    @pl.when(at_home)
    def _():
        sent(o_tx.at[pl.ds(0, GROUP + 4 - 2)], o_send)

    @pl.when(jnp.logical_not(at_home))
    def _():
        sent(o_tx.at[pl.ds(0, GROUP + 4 - 1)], o_send)

    keep_copy.wait()
    pass_on.wait()


def body(*args):
    hbm = pl.BlockSpec(memory_space=pltpu.HBM)
    out = jax.ShapeDtypeStruct((1, IMAGES, 1, W, C), BF16)
    dma = pltpu.SemaphoreType.DMA
    return pl.pallas_call(
        kernel,
        out_shape=(out, out),
        in_specs=[hbm] * 13,
        out_specs=(hbm, hbm),
        scratch_shapes=[
            pltpu.SMEM((1,), jnp.int32),
            pltpu.VMEM((5, 1, C), F32),
            pltpu.VMEM((3, IMAGES, W, C), BF16),
            pltpu.VMEM((3, 3, C, C), BF16),
            pltpu.VMEM((TEMB, C), BF16),
            pltpu.VMEM((C, C), BF16),
            pltpu.VMEM((C, C), BF16),
            pltpu.VMEM((C, C), BF16),
            pltpu.VMEM((C, C), BF16),
            pltpu.VMEM((8, LANES), F32),
            pltpu.VMEM((GROUP, 8, LANES), F32),
            pltpu.VMEM((X, 8, LANES), F32),
            pltpu.VMEM((IMAGES, 3, W + 16, C), F32),
            pltpu.VMEM((IMAGES * W, 9 * C), BF16),
            pltpu.VMEM((IMAGES * W, C), BF16),
            pltpu.VMEM((IMAGES, Z, 96, LANES), BF16),
            pltpu.VMEM((IMAGES, 2, W, LANES), BF16),
            pltpu.VMEM((IMAGES, 2, W // 2, LANES), BF16),
            pltpu.VMEM((GROUP, 96, LANES), BF16),
            pltpu.VMEM((GROUP, W, LANES), BF16),
            pltpu.VMEM((X, 4, W // 2, LANES), BF16),
            pltpu.VMEM((X, GROUP, W, LANES), BF16),
            pltpu.VMEM((KEYS, LANES), BF16),
            pltpu.VMEM((KEYS, LANES), BF16),
            pltpu.VMEM((KEYS, LANES), F32),
            pltpu.VMEM((KEYS, LANES), F32),
            pltpu.VMEM((X - 1, QB, LANES), BF16),
            pltpu.VMEM((X, QB, LANES), BF16),
            pltpu.VMEM((GROUP + 4, W // 2, LANES), BF16),
            pltpu.VMEM((IMAGES, HEADS, W // 2, LANES), BF16),
            pltpu.VMEM((IMAGES * W, C), BF16),
            pltpu.VMEM((IMAGES, W, C), BF16),
            dma,
            dma((6,)),
            dma((2,)),
            dma((2,)),
            dma((2,)),
            dma((2,)),
            dma,
            dma((GROUP,)),
            dma,
            dma,
            dma((4,)),
            dma((X,)),
            dma,
            dma((X,)),
            dma,
            dma((X - 1,)),
            dma,
            dma,
            dma,
            dma,
            dma,
            dma,
            dma((6,)),
        ],
        compiler_params=pltpu.CompilerParams(
            collective_id=0, has_side_effects=True, vmem_limit_bytes=63 * 1024 * 1024
        ),
    )(*args)


def solution(mesh):
    placed = (
        P(),
        P("section", None, "patch", None, None),
        P("section", None, None, None, None),
        P("section", None),
        P("section", None),
        P("section", None),
        P("section", None, None),
        P("section", None),
        P("section", None),
        P("section", None, None),
        P("section", None, None),
        P("section", None, None),
        P("section", None, None),
    )
    whole = P("section", None, "patch", None, None)
    return jax.shard_map(body, mesh=mesh, in_specs=placed, out_specs=(whole, whole), check_vma=False)
```

```python
import functools
import math

import jax
import jax.numpy as jnp
from jax import lax
from jax.experimental import pallas as pl
from jax.experimental.pallas import tpu as pltpu
from jax.sharding import PartitionSpec as P

GROUPS = 32
HEAD_DIM = 64
HEADS = 10
C = 640
W = 64
H = 64
IMAGES = 2
TEMB = 320
PER = C // GROUPS
LANES = 128
X = 4
Z = 8
GROUP = 16
KEYS = GROUP * W
QB = 256
F32 = jnp.float32
BF16 = jnp.bfloat16


def thirds(value):
    hi = value.astype(BF16).astype(F32)
    mid = (value - hi).astype(BF16).astype(F32)
    lo = (value - hi - mid).astype(BF16).astype(F32)
    return hi, mid, lo


def exact_dot(value, matrix):
    parts = jnp.concatenate([*thirds(value), jnp.zeros_like(value)], axis=0).astype(BF16)
    out = jnp.dot(parts, matrix, preferred_element_type=F32)
    return out[0:8] + out[8:16] + out[16:24]


def rolled(value):
    return pltpu.roll(value, HEAD_DIM, 1)


def lanes_of(shape):
    return lax.broadcasted_iota(jnp.int32, shape, 1)


def kernel(
    ts_hbm, x_hbm, ck_hbm, cb_hbm, gg_hbm, gb_hbm, tw_hbm, ng_hbm, nb_hbm, wq_hbm, wk_hbm, wv_hbm, wo_hbm,
    out_hbm,
    ts_ref, vectors, xin, wc, wt, wq, wk, wv, wo,
    stat_tx, stat_rx, stat2_rx, pad, patches, resid_s,
    send_kv, send_qm, send_b, send_q, recv_kv, recv_qm, recv_b, recv_q, kvx, q_main, q_extra,
    m_s, acc_s, part_tx, part_rx, o_tx, o_rx, att, fresh_s,
    x_sem, w_sem, st_send, st_recv, halo_send, halo_recv,
    a_send, a_recv, qm_recv, b_send, b_recv, q_send, q_recv, f_send, f_recv, qf_send, p_send, p_recv, o_send, o_recv,
    out_sem, h_send, h_recv, v_sem,
):
    me = lax.axis_index("patch")
    sec = lax.axis_index("section")
    my_y = me // (X * Z)
    my_x = (me // Z) % X
    my_z = me % Z
    my_i = my_y * Z + my_z

    def at(y, x, z):
        return {"patch": y * (X * Z) + x * Z + z}

    def sent(ref, sem):
        pltpu.make_async_copy(ref, ref, sem).wait()

    x_copy = pltpu.make_async_copy(x_hbm.at[0, :, 0], xin.at[1], x_sem)
    x_copy.start()
    loads = [
        pltpu.make_async_copy(tw_hbm.at[0], wt, w_sem.at[0]),
        pltpu.make_async_copy(ck_hbm.at[0], wc, w_sem.at[1]),
        pltpu.make_async_copy(wq_hbm.at[0], wq, w_sem.at[2]),
        pltpu.make_async_copy(wk_hbm.at[0], wk, w_sem.at[3]),
        pltpu.make_async_copy(wv_hbm.at[0], wv, w_sem.at[4]),
        pltpu.make_async_copy(wo_hbm.at[0], wo, w_sem.at[5]),
    ]
    small = [
        pltpu.make_async_copy(ref, vectors.at[n], v_sem.at[n])
        for n, ref in enumerate((cb_hbm, gg_hbm, gb_hbm, ng_hbm, nb_hbm))
    ]
    small.append(pltpu.make_async_copy(ts_hbm, ts_ref, v_sem.at[5]))
    for load in [*small, loads[0]]:
        load.start()

    barrier = pltpu.get_barrier_semaphore()

    def greet(device):
        pl.semaphore_signal(barrier, inc=1, device_id=device, device_id_type=pl.DeviceIdType.MESH)

    @pl.loop(1, GROUP)
    def _(k):
        i = (my_i + k) % GROUP
        greet(at(i // Z, my_x, i % Z))

    for k in range(1, X):
        greet(at(my_y, (my_x + k) % X, my_z))
    greet({"patch": (me + 1) % H})
    greet({"patch": (me + H - 1) % H})
    greet({"section": (sec + 1) % 4})
    greet({"section": (sec + 3) % 4})

    channel = lax.broadcasted_iota(jnp.int32, (C, LANES), 0)
    group = lax.broadcasted_iota(jnp.int32, (C, LANES), 1)
    gather = ((channel >= group * PER) & (channel < (group + 1) * PER)).astype(F32).astype(BF16)
    group_t = lax.broadcasted_iota(jnp.int32, (LANES, C), 0)
    channel_t = lax.broadcasted_iota(jnp.int32, (LANES, C), 1)
    spread = ((channel_t >= group_t * PER) & (channel_t < (group_t + 1) * PER)).astype(F32).astype(BF16)
    x_copy.wait()
    mine = xin[1].astype(F32)
    sums = [jnp.sum(mine[b], axis=0, keepdims=True) for b in range(IMAGES)]
    squares = [jnp.sum(mine[b] * mine[b], axis=0, keepdims=True) for b in range(IMAGES)]
    stacked = jnp.concatenate([*sums, *squares, jnp.zeros((4, C), F32)], axis=0)
    own_stats = exact_dot(stacked, gather)
    stat_tx[...] = own_stats
    stat_rx[my_i] = own_stats

    pl.semaphore_wait(barrier, GROUP - 1 + X - 1 + 4)

    @pl.loop(1, GROUP)
    def _(k):
        i = (my_i + k) % GROUP
        pltpu.make_async_remote_copy(
            stat_tx, stat_rx.at[my_i], st_send.at[0], st_recv.at[0], device_id=at(i // Z, my_x, i % Z)
        ).start()

    below = pltpu.make_async_remote_copy(
        xin.at[1], xin.at[0], halo_send.at[0], halo_recv.at[0], device_id={"patch": (me + 1) % H}
    )
    above = pltpu.make_async_remote_copy(
        xin.at[1], xin.at[2], halo_send.at[1], halo_recv.at[1], device_id={"patch": (me + H - 1) % H}
    )
    below.start()
    above.start()

    for load in loads[1:]:
        load.start()

    half = TEMB // 2
    place = lax.broadcasted_iota(jnp.int32, (8, TEMB), 1)
    step = jnp.where(place < half, place, place - half).astype(F32)
    for load in small:
        load.wait()
    angle = ts_ref[0].astype(F32) * jnp.exp(step * (-math.log(10000.0) / half))
    tembed = jnp.where(place < half, jnp.cos(angle), jnp.sin(angle))
    loads[0].wait()
    tproj = exact_dot(tembed * jax.nn.sigmoid(tembed), wt[...])[0:1]
    constant = tproj + vectors[0]

    fifteen = stat_rx.at[pl.ds(0, GROUP - 1)]
    sent(fifteen, st_recv.at[0])
    column_stats = jnp.sum(stat_rx[...], axis=0)
    stat2_rx[my_x] = column_stats
    for k in (1, 3, 2):
        pltpu.make_async_remote_copy(
            stat2_rx.at[my_x], stat2_rx.at[my_x], st_send.at[1], st_recv.at[1],
            device_id=at(my_y, (my_x + k) % X, my_z),
        ).start()
    three = stat2_rx.at[pl.ds(0, X - 1)]
    sent(three, st_recv.at[1])
    stats = jnp.sum(stat2_rx[...], axis=0) * (1.0 / (H * W * PER))
    mean = stats[0:2]
    rstd = lax.rsqrt(stats[2:4] - mean * mean + 1e-05)
    wide = exact_dot(jnp.concatenate([mean, rstd, jnp.zeros((4, LANES), F32)], axis=0), spread)
    scale = wide[2:4] * vectors[1]
    shift = vectors[2] - wide[0:2] * scale

    below.wait_recv()
    above.wait_recv()
    keep = [(me > 0).astype(F32), 1.0, (me < H - 1).astype(F32)]
    edge = jnp.zeros((8, C), F32)
    for b in range(IMAGES):
        for di in range(3):
            line = xin[di, b].astype(F32) * scale[b : b + 1] + shift[b : b + 1]
            line = line * jax.nn.sigmoid(line)
            if di != 1:
                line = line * keep[di]
            pad[b, di, 0:8] = edge
            pad[b, di, 72:80] = edge
            pad[b, di, 8:72] = line
            for dj in range(3):
                tap = di * 3 + dj
                patches[b * W : (b + 1) * W, tap * C : (tap + 1) * C] = pad[b, di, 7 + dj : 71 + dj].astype(BF16)
    loads[1].wait()
    conv = jnp.dot(patches[...], wc[...].reshape(9 * C, C), preferred_element_type=F32)
    resid = (xin[1].astype(F32).reshape(IMAGES * W, C) + conv + constant).astype(BF16)
    resid_s[...] = resid
    r32 = resid.astype(F32)
    centre = jnp.mean(r32, axis=-1, keepdims=True)
    off = r32 - centre
    lvar = jnp.mean(off * off, axis=-1, keepdims=True)
    normed = (off * lax.rsqrt(lvar + 1e-05) * vectors[3] + vectors[4]).astype(BF16)

    left = lanes_of((W, LANES)) < HEAD_DIM
    left_half = lanes_of((W // 2, LANES)) < HEAD_DIM
    for load in loads[2:5]:
        load.wait()
    queries = jnp.dot(normed, wq[...], preferred_element_type=F32) * (HEAD_DIM**-0.5)
    keys = jnp.dot(normed, wk[...], preferred_element_type=F32)
    values = jnp.dot(normed, wv[...], preferred_element_type=F32)
    for b in range(IMAGES):
        rows = slice(b * W, (b + 1) * W)
        for j in range(HEADS // 2):
            lanes = slice(j * LANES, (j + 1) * LANES)
            k_pair, v_pair, q_pair = keys[rows, lanes], values[rows, lanes], queries[rows, lanes]
            top, bottom = q_pair[: W // 2], q_pair[W // 2 :]
            kv = (jnp.where(left, k_pair, rolled(v_pair)), jnp.where(left, rolled(k_pair), v_pair))
            qq = (jnp.where(left_half, top, rolled(bottom)), jnp.where(left_half, rolled(top), bottom))
            for e in range(2):
                head = 2 * j + e
                if head < Z:
                    send_qm[b, head] = qq[e].astype(BF16)
                    send_kv[b, head] = kv[e].astype(BF16)
                else:
                    send_q[b * 2 + head - Z] = qq[e].astype(BF16)
                    send_b[b * 2 + head - Z] = kv[e].astype(BF16)

    def partner(k):
        m = k // 2
        odd = m % 2
        dz = odd * ((m + 1) // 2) + (1 - odd) * ((Z - m // 2) % Z)
        return (my_y + k % 2) % 2, dz

    def to_group(k, source, target, send_sem, recv_sem):
        b, dz = partner(k)
        z = (my_z + dz) % Z

        @pl.when(k == 0)
        def _():
            pltpu.make_async_copy(source(b, z), target, recv_sem).start()

        @pl.when(k > 0)
        def _():
            pltpu.make_async_remote_copy(
                source(b, z), target, send_sem, recv_sem, device_id=at(b, my_x, z)
            ).start()

    own_pair = my_z // 2
    for d in range(4):
        pair = (own_pair + d) % 4
        source, target = send_q.at[pair], recv_q.at[my_x, own_pair]
        if d == 0:
            pltpu.make_async_copy(source, target, q_recv.at[my_x]).start()
        else:
            pltpu.make_async_remote_copy(
                source, target, q_send, q_recv.at[my_x], device_id=at(my_y, my_x, 2 * pair + my_z % 2)
            ).start()

    pltpu.make_async_copy(send_b.at[own_pair], recv_b.at[my_y, my_z], b_recv.at[0]).start()

    @pl.loop(1, Z)
    def _(k):
        odd = k % 2
        z = (my_z + odd * ((k + 1) // 2) + (1 - odd) * (Z - k // 2)) % Z
        pltpu.make_async_remote_copy(
            send_b.at[z // 2], recv_b.at[my_y, my_z], b_send.at[0], b_recv.at[0], device_id=at(my_y, my_x, z)
        ).start()

    @pl.loop(0, GROUP)
    def _(k):
        to_group(k, lambda b, z: send_kv.at[b, z], recv_kv.at[my_i], a_send.at[0], a_recv.at[my_i])

    @pl.loop(0, GROUP)
    def _(k):
        to_group(k, lambda b, z: send_qm.at[b, z], recv_qm.at[my_i], a_send.at[1], qm_recv)

    sent(recv_q.at[my_x], q_recv.at[my_x])
    for d in (1, 3, 2):
        pltpu.make_async_remote_copy(
            recv_q.at[my_x], recv_q.at[my_x], qf_send, q_recv.at[my_x],
            device_id=at(my_y, (my_x + d) % X, my_z),
        ).start()
    sent(recv_b.at[my_y], b_recv.at[0])
    across = pltpu.make_async_remote_copy(
        recv_b.at[my_y], recv_b.at[my_y], b_send.at[1], b_recv.at[1], device_id=at(1 - my_y, my_x, my_z)
    )
    across.start()

    @pl.loop(0, GROUP)
    def _(k):
        y, dz = partner(k)
        z = (my_z + Z - dz) % Z
        i = y * Z + z
        sent(recv_kv.at[i], a_recv.at[i])
        for d in (1, 3, 2):
            pltpu.make_async_remote_copy(
                recv_kv.at[i], kvx.at[d - 1, i], f_send, f_recv.at[d - 1], device_id=at(my_y, (my_x + d) % X, my_z)
            ).start()

    def unpack(packed, out, base):
        wide = packed.astype(F32)
        out[pl.ds(base, 32)] = jnp.where(left_half, wide, 0.0).astype(BF16)
        out[pl.ds(base + 32, 32)] = jnp.where(left_half, rolled(wide), 0.0).astype(BF16)

    def rows_of(n):
        return slice(n * QB, (n + 1) * QB)

    lane_k = lanes_of((KEYS, LANES))

    def score_of(q, kv):
        return lax.dot_general(q, kv, (((1,), (1,)), ((), ())), preferred_element_type=F32)

    def softened(score, old):
        pieces = [score[:, i * LANES : (i + 1) * LANES] for i in range(KEYS // LANES)]
        top = jnp.max(functools.reduce(jnp.maximum, pieces), axis=-1, keepdims=True)
        top = jnp.broadcast_to(top, (QB, LANES))
        if old is not None:
            top = jnp.maximum(old, top)
        probs = jnp.concatenate([jnp.exp(piece - top).astype(BF16) for piece in pieces], axis=1)
        return top, probs, None if old is None else jnp.exp(old - top)

    def attend(kv, queries, old_tops, old_sums, done):
        ones_values = jnp.where(lane_k < HEAD_DIM, 1.0, kv.astype(F32)).astype(BF16)
        blocks = KEYS // QB
        score = score_of(queries(0), kv)
        for n in range(blocks):
            following = score_of(queries(n + 1), kv) if n + 1 < blocks else None
            top, probs, fade = softened(score, None if old_tops is None else old_tops(n))
            out = jnp.dot(probs, ones_values, preferred_element_type=F32)
            if fade is not None:
                out = out + fade * old_sums(n)
            done(n, top, out)
            score = following

    def main_queries(n):
        return q_main[rows_of(n)]

    def main_tops(n):
        return m_s[rows_of(n)]

    def main_sums(n):
        return acc_s[rows_of(n)]

    def keep_main(n, top, out):
        m_s[rows_of(n)] = top
        acc_s[rows_of(n)] = out

    for d in (1, 3, 2):
        c = (my_x + d) % X
        sent(recv_q.at[c], q_recv.at[c])
    sent(recv_b.at[my_y], b_recv.at[1])

    @pl.loop(0, GROUP)
    def _(i):
        unpack(recv_q[i // 4, i % 4], q_extra, pl.multiple_of(i * W, W))

    lanes_q = lanes_of((QB, LANES))

    def extra_queries(n):
        c = (my_x + n + 1) % X
        return q_extra[pl.ds(pl.multiple_of(c * QB, QB), QB)]

    def extra_done(n, top, out):
        total = out[:, 0:1]
        hi, mid, lo = thirds(top + jnp.log(total))
        lse = jnp.where(lanes_q < 16, hi, jnp.where(lanes_q < 32, mid, lo))
        packed = jnp.where(lanes_q < HEAD_DIM, lse, out / total).astype(BF16)
        if n < X - 1:
            part_tx[n] = packed
            pltpu.make_async_remote_copy(
                part_tx.at[n], part_rx.at[my_x], p_send.at[n], p_recv, device_id=at(my_y, (my_x + n + 1) % X, my_z)
            ).start()
        else:
            part_rx[my_x] = packed

    attend(recv_b[...].reshape(KEYS, LANES), extra_queries, None, None, extra_done)

    sent(recv_qm, qm_recv)

    @pl.loop(0, GROUP)
    def _(i):
        unpack(recv_qm[i], q_main, pl.multiple_of(i * W, W))

    attend(recv_kv[...].reshape(KEYS, LANES), main_queries, None, None, keep_main)
    for d in (1, 3):
        sent(kvx.at[d - 1], f_recv.at[d - 1])
        attend(kvx[d - 1].reshape(KEYS, LANES), main_queries, main_tops, main_sums, keep_main)

    def pack_rows(out, r):
        top, bottom = out[r * W : r * W + 32], out[r * W + 32 : (r + 1) * W]
        return jnp.where(left_half, rolled(top), bottom).astype(BF16)

    def home(slot, i, image, head):
        y, z = i // Z, i % Z

        @pl.when(i == my_i)
        def _():
            pltpu.make_async_copy(o_tx.at[slot], o_rx.at[image, head], o_recv).start()

        @pl.when(i != my_i)
        def _():
            pltpu.make_async_remote_copy(
                o_tx.at[slot], o_rx.at[image, head], o_send, o_recv, device_id=at(y, my_x, z)
            ).start()

    sent(part_rx.at[pl.ds(0, X - 1)], p_recv)
    parts = [part_rx[c].astype(F32) for c in range(X)]
    lses = [p[:, 0:1] + p[:, 16:17] + p[:, 32:33] for p in parts]
    peak = functools.reduce(jnp.maximum, lses)
    weights = [jnp.exp(lse - peak) for lse in lses]
    merged = sum(w * p for w, p in zip(weights, parts)) / sum(weights)
    for r in range(4):
        o_tx[GROUP + r] = pack_rows(merged, r)
    for r in range(4):
        home(GROUP + r, my_y * Z + 2 * r + my_z % 2, my_z // 4, Z + own_pair % 2)

    sent(kvx.at[1], f_recv.at[1])

    def main_done(n, top, out):
        out = out / out[:, 0:1]
        for r in range(QB // W):
            o_tx[n * (QB // W) + r] = pack_rows(out, r)
        for r in range(QB // W):
            home(n * (QB // W) + r, n * (QB // W) + r, my_y, my_z)

    attend(kvx[1].reshape(KEYS, LANES), main_queries, main_tops, main_sums, main_done)

    sent(o_rx, o_recv)
    for b in range(IMAGES):
        for j in range(HEADS // 2):
            even, odd = o_rx[b, 2 * j].astype(F32), o_rx[b, 2 * j + 1].astype(F32)
            att[b * W : b * W + 32, j * LANES : (j + 1) * LANES] = jnp.where(left_half, even, rolled(odd)).astype(BF16)
            att[b * W + 32 : (b + 1) * W, j * LANES : (j + 1) * LANES] = jnp.where(
                left_half, rolled(even), odd
            ).astype(BF16)
    loads[5].wait()
    mixed = jnp.dot(att[...], wo[...], preferred_element_type=F32)
    fresh_s[...] = (resid_s[...].astype(F32) + mixed).astype(BF16).reshape(IMAGES, W, C)
    pass_on = pltpu.make_async_remote_copy(
        fresh_s, out_hbm.at[1], h_send, h_recv, device_id={"section": (sec + 1) % 4}
    )
    pass_on.start()
    keep_copy = pltpu.make_async_copy(fresh_s, out_hbm.at[0], out_sem)
    keep_copy.start()

    below.wait_send()
    above.wait_send()
    sent(fifteen, st_send.at[0])
    sent(three, st_send.at[1])
    sent(recv_kv.at[pl.ds(0, GROUP - 1)], a_send.at[0])
    sent(recv_qm.at[pl.ds(0, GROUP - 1)], a_send.at[1])
    sent(recv_b.at[0, pl.ds(0, Z - 1)], b_send.at[0])
    across.wait_send()
    sent(send_q.at[pl.ds(0, 3)], q_send)
    sent(kvx, f_send)
    sent(recv_q.at[pl.ds(0, X - 1)], qf_send)
    for t in range(X - 1):
        sent(part_tx.at[t], p_send.at[t])
    sent(o_tx.at[pl.ds(0, GROUP + 4 - 2)], o_send)
    keep_copy.wait()
    pass_on.wait()


def body(*args):
    hbm = pl.BlockSpec(memory_space=pltpu.HBM)
    out = jax.ShapeDtypeStruct((2, IMAGES, W, C), BF16)
    dma = pltpu.SemaphoreType.DMA
    both = pl.pallas_call(
        kernel,
        out_shape=out,
        in_specs=[hbm] * 13,
        out_specs=hbm,
        scratch_shapes=[
            pltpu.SMEM((1,), jnp.int32),
            pltpu.VMEM((5, 1, C), F32),
            pltpu.VMEM((3, IMAGES, W, C), BF16),
            pltpu.VMEM((3, 3, C, C), BF16),
            pltpu.VMEM((TEMB, C), BF16),
            pltpu.VMEM((C, C), BF16),
            pltpu.VMEM((C, C), BF16),
            pltpu.VMEM((C, C), BF16),
            pltpu.VMEM((C, C), BF16),
            pltpu.VMEM((8, LANES), F32),
            pltpu.VMEM((GROUP, 8, LANES), F32),
            pltpu.VMEM((X, 8, LANES), F32),
            pltpu.VMEM((IMAGES, 3, W + 16, C), F32),
            pltpu.VMEM((IMAGES * W, 9 * C), BF16),
            pltpu.VMEM((IMAGES * W, C), BF16),
            pltpu.VMEM((IMAGES, Z, W, LANES), BF16),
            pltpu.VMEM((IMAGES, Z, W // 2, LANES), BF16),
            pltpu.VMEM((4, W, LANES), BF16),
            pltpu.VMEM((4, W // 2, LANES), BF16),
            pltpu.VMEM((GROUP, W, LANES), BF16),
            pltpu.VMEM((GROUP, W // 2, LANES), BF16),
            pltpu.VMEM((2, Z, W, LANES), BF16),
            pltpu.VMEM((X, 4, W // 2, LANES), BF16),
            pltpu.VMEM((X - 1, GROUP, W, LANES), BF16),
            pltpu.VMEM((KEYS, LANES), BF16),
            pltpu.VMEM((KEYS, LANES), BF16),
            pltpu.VMEM((KEYS, LANES), F32),
            pltpu.VMEM((KEYS, LANES), F32),
            pltpu.VMEM((X - 1, QB, LANES), BF16),
            pltpu.VMEM((X, QB, LANES), BF16),
            pltpu.VMEM((GROUP + 4, W // 2, LANES), BF16),
            pltpu.VMEM((IMAGES, HEADS, W // 2, LANES), BF16),
            pltpu.VMEM((IMAGES * W, C), BF16),
            pltpu.VMEM((IMAGES, W, C), BF16),
            dma,
            dma((6,)),
            dma((2,)),
            dma((2,)),
            dma((2,)),
            dma((2,)),
            dma((2,)),
            dma((GROUP,)),
            dma,
            dma((2,)),
            dma((2,)),
            dma,
            dma((X,)),
            dma,
            dma((X - 1,)),
            dma,
            dma((X - 1,)),
            dma,
            dma,
            dma,
            dma,
            dma,
            dma,
            dma((6,)),
        ],
        compiler_params=pltpu.CompilerParams(
            collective_id=0, has_side_effects=True, vmem_limit_bytes=63 * 1024 * 1024
        ),
    )(*args)
    whole = (1, IMAGES, 1, W, C)
    return both[0].reshape(whole), both[1].reshape(whole)


def solution(mesh):
    placed = (
        P(),
        P("section", None, "patch", None, None),
        P("section", None, None, None, None),
        P("section", None),
        P("section", None),
        P("section", None),
        P("section", None, None),
        P("section", None),
        P("section", None),
        P("section", None, None),
        P("section", None, None),
        P("section", None, None),
        P("section", None, None),
    )
    whole = P("section", None, "patch", None, None)
    return jax.shard_map(body, mesh=mesh, in_specs=placed, out_specs=(whole, whole), check_vma=False)
```

```python
import functools
import math

import jax
import jax.numpy as jnp
from jax import lax
from jax.experimental import pallas as pl
from jax.experimental.pallas import tpu as pltpu
from jax.sharding import PartitionSpec as P

GROUPS = 32
HEAD_DIM = 64
HEADS = 10
C = 640
W = 64
H = 64
IMAGES = 2
TEMB = 320
PER = C // GROUPS
LANES = 128
X = 4
Z = 8
GROUP = 16
KEYS = GROUP * W
QB = 256
F32 = jnp.float32
BF16 = jnp.bfloat16


def thirds(value):
    hi = value.astype(BF16).astype(F32)
    mid = (value - hi).astype(BF16).astype(F32)
    lo = (value - hi - mid).astype(BF16).astype(F32)
    return hi, mid, lo


def exact_dot(value, matrix):
    parts = jnp.concatenate([*thirds(value), jnp.zeros_like(value)], axis=0).astype(BF16)
    out = jnp.dot(parts, matrix, preferred_element_type=F32)
    return out[0:8] + out[8:16] + out[16:24]


def rolled(value):
    return pltpu.roll(value, HEAD_DIM, 1)


def lanes_of(shape):
    return lax.broadcasted_iota(jnp.int32, shape, 1)


def kernel(
    ts_hbm, x_hbm, ck_hbm, cb_hbm, gg_hbm, gb_hbm, tw_hbm, ng_hbm, nb_hbm, wq_hbm, wk_hbm, wv_hbm, wo_hbm,
    out_hbm,
    ts_ref, vectors, xin, wc, wt, wq, wk, wv, wo,
    stat_tx, stat_rx, stat2_rx, pad, patches, resid_s,
    send_kv, send_qm, send_b, send_q, recv_kv, recv_qm, recv_b, recv_q, kvx, q_main, q_extra,
    m_s, acc_s, part_tx, part_rx, o_tx, o_rx, att, fresh_s,
    x_sem, w_sem, st_send, st_recv, halo_send, halo_recv,
    a_send, a_recv, qm_recv, b_send, b_recv, q_send, q_recv, f_send, f_recv, qf_send, p_send, p_recv, o_send, o_recv,
    out_sem, h_send, h_recv, v_sem,
):
    me = lax.axis_index("patch")
    sec = lax.axis_index("section")
    my_y = me // (X * Z)
    my_x = (me // Z) % X
    my_z = me % Z
    my_i = my_y * Z + my_z

    def at(y, x, z):
        return {"patch": y * (X * Z) + x * Z + z}

    def sent(ref, sem):
        pltpu.make_async_copy(ref, ref, sem).wait()

    x_copy = pltpu.make_async_copy(x_hbm.at[0, :, 0], xin.at[1], x_sem)
    x_copy.start()
    loads = [
        pltpu.make_async_copy(tw_hbm.at[0], wt, w_sem.at[0]),
        pltpu.make_async_copy(ck_hbm.at[0], wc, w_sem.at[1]),
        pltpu.make_async_copy(wq_hbm.at[0], wq, w_sem.at[2]),
        pltpu.make_async_copy(wk_hbm.at[0], wk, w_sem.at[3]),
        pltpu.make_async_copy(wv_hbm.at[0], wv, w_sem.at[4]),
        pltpu.make_async_copy(wo_hbm.at[0], wo, w_sem.at[5]),
    ]
    small = [
        pltpu.make_async_copy(ref, vectors.at[n], v_sem.at[n])
        for n, ref in enumerate((cb_hbm, gg_hbm, gb_hbm, ng_hbm, nb_hbm))
    ]
    small.append(pltpu.make_async_copy(ts_hbm, ts_ref, v_sem.at[5]))
    for load in [*small, loads[0]]:
        load.start()

    barrier = pltpu.get_barrier_semaphore()

    def greet(device):
        pl.semaphore_signal(barrier, inc=1, device_id=device, device_id_type=pl.DeviceIdType.MESH)

    @pl.loop(1, GROUP)
    def _(k):
        i = (my_i + k) % GROUP
        greet(at(i // Z, my_x, i % Z))

    for k in range(1, X):
        greet(at(my_y, (my_x + k) % X, my_z))
    greet({"patch": (me + 1) % H})
    greet({"patch": (me + H - 1) % H})
    greet({"section": (sec + 1) % 4})
    greet({"section": (sec + 3) % 4})

    channel = lax.broadcasted_iota(jnp.int32, (C, LANES), 0)
    group = lax.broadcasted_iota(jnp.int32, (C, LANES), 1)
    gather = ((channel >= group * PER) & (channel < (group + 1) * PER)).astype(F32).astype(BF16)
    group_t = lax.broadcasted_iota(jnp.int32, (LANES, C), 0)
    channel_t = lax.broadcasted_iota(jnp.int32, (LANES, C), 1)
    spread = ((channel_t >= group_t * PER) & (channel_t < (group_t + 1) * PER)).astype(F32).astype(BF16)
    x_copy.wait()
    mine = xin[1].astype(F32)
    sums = [jnp.sum(mine[b], axis=0, keepdims=True) for b in range(IMAGES)]
    squares = [jnp.sum(mine[b] * mine[b], axis=0, keepdims=True) for b in range(IMAGES)]
    stacked = jnp.concatenate([*sums, *squares, jnp.zeros((4, C), F32)], axis=0)
    own_stats = exact_dot(stacked, gather)
    stat_tx[...] = own_stats
    stat_rx[my_i] = own_stats

    pl.semaphore_wait(barrier, GROUP - 1 + X - 1 + 4)

    @pl.loop(1, GROUP)
    def _(k):
        i = (my_i + k) % GROUP
        pltpu.make_async_remote_copy(
            stat_tx, stat_rx.at[my_i], st_send.at[0], st_recv.at[0], device_id=at(i // Z, my_x, i % Z)
        ).start()

    below = pltpu.make_async_remote_copy(
        xin.at[1], xin.at[0], halo_send.at[0], halo_recv.at[0], device_id={"patch": (me + 1) % H}
    )
    above = pltpu.make_async_remote_copy(
        xin.at[1], xin.at[2], halo_send.at[1], halo_recv.at[1], device_id={"patch": (me + H - 1) % H}
    )
    below.start()
    above.start()

    for load in loads[1:]:
        load.start()

    half = TEMB // 2
    place = lax.broadcasted_iota(jnp.int32, (8, TEMB), 1)
    step = jnp.where(place < half, place, place - half).astype(F32)
    for load in small:
        load.wait()
    angle = ts_ref[0].astype(F32) * jnp.exp(step * (-math.log(10000.0) / half))
    tembed = jnp.where(place < half, jnp.cos(angle), jnp.sin(angle))
    loads[0].wait()
    tproj = exact_dot(tembed * jax.nn.sigmoid(tembed), wt[...])[0:1]
    constant = tproj + vectors[0]

    fifteen = stat_rx.at[pl.ds(0, GROUP - 1)]
    sent(fifteen, st_recv.at[0])
    column_stats = jnp.sum(stat_rx[...], axis=0)
    stat2_rx[my_x] = column_stats
    for k in (1, 3, 2):
        pltpu.make_async_remote_copy(
            stat2_rx.at[my_x], stat2_rx.at[my_x], st_send.at[1], st_recv.at[1],
            device_id=at(my_y, (my_x + k) % X, my_z),
        ).start()
    three = stat2_rx.at[pl.ds(0, X - 1)]
    sent(three, st_recv.at[1])
    stats = jnp.sum(stat2_rx[...], axis=0) * (1.0 / (H * W * PER))
    mean = stats[0:2]
    rstd = lax.rsqrt(stats[2:4] - mean * mean + 1e-05)
    wide = exact_dot(jnp.concatenate([mean, rstd, jnp.zeros((4, LANES), F32)], axis=0), spread)
    scale = wide[2:4] * vectors[1]
    shift = vectors[2] - wide[0:2] * scale

    below.wait_recv()
    above.wait_recv()
    keep = [(me > 0).astype(F32), 1.0, (me < H - 1).astype(F32)]
    edge = jnp.zeros((8, C), F32)
    for b in range(IMAGES):
        for di in range(3):
            line = xin[di, b].astype(F32) * scale[b : b + 1] + shift[b : b + 1]
            line = line * jax.nn.sigmoid(line)
            if di != 1:
                line = line * keep[di]
            pad[b, di, 0:8] = edge
            pad[b, di, 72:80] = edge
            pad[b, di, 8:72] = line
            for dj in range(3):
                tap = di * 3 + dj
                patches[b * W : (b + 1) * W, tap * C : (tap + 1) * C] = pad[b, di, 7 + dj : 71 + dj].astype(BF16)
    loads[1].wait()
    conv = jnp.dot(patches[...], wc[...].reshape(9 * C, C), preferred_element_type=F32)
    resid = (xin[1].astype(F32).reshape(IMAGES * W, C) + conv + constant).astype(BF16)
    resid_s[...] = resid
    r32 = resid.astype(F32)
    centre = jnp.mean(r32, axis=-1, keepdims=True)
    off = r32 - centre
    lvar = jnp.mean(off * off, axis=-1, keepdims=True)
    normed = (off * lax.rsqrt(lvar + 1e-05) * vectors[3] + vectors[4]).astype(BF16)

    left = lanes_of((W, LANES)) < HEAD_DIM
    left_half = lanes_of((W // 2, LANES)) < HEAD_DIM
    for load in loads[2:5]:
        load.wait()
    queries = jnp.dot(normed, wq[...], preferred_element_type=F32) * (HEAD_DIM**-0.5)
    keys = jnp.dot(normed, wk[...], preferred_element_type=F32)
    values = jnp.dot(normed, wv[...], preferred_element_type=F32)
    for b in range(IMAGES):
        rows = slice(b * W, (b + 1) * W)
        for j in range(HEADS // 2):
            lanes = slice(j * LANES, (j + 1) * LANES)
            k_pair, v_pair, q_pair = keys[rows, lanes], values[rows, lanes], queries[rows, lanes]
            top, bottom = q_pair[: W // 2], q_pair[W // 2 :]
            kv = (jnp.where(left, k_pair, rolled(v_pair)), jnp.where(left, rolled(k_pair), v_pair))
            qq = (jnp.where(left_half, top, rolled(bottom)), jnp.where(left_half, rolled(top), bottom))
            for e in range(2):
                head = 2 * j + e
                if head < Z:
                    send_qm[b, head] = qq[e].astype(BF16)
                    send_kv[b, head] = kv[e].astype(BF16)
                else:
                    send_q[b * 2 + head - Z] = qq[e].astype(BF16)
                    send_b[b * 2 + head - Z] = kv[e].astype(BF16)

    def partner(k):
        m = k // 2
        odd = m % 2
        dz = odd * ((m + 1) // 2) + (1 - odd) * ((Z - m // 2) % Z)
        return (my_y + k % 2) % 2, dz

    def to_group(k, source, target, send_sem, recv_sem):
        b, dz = partner(k)
        z = (my_z + dz) % Z

        @pl.when(k == 0)
        def _():
            pltpu.make_async_copy(source(b, z), target, recv_sem).start()

        @pl.when(k > 0)
        def _():
            pltpu.make_async_remote_copy(
                source(b, z), target, send_sem, recv_sem, device_id=at(b, my_x, z)
            ).start()

    own_pair = my_z // 2
    for d in range(4):
        pair = (own_pair + d) % 4
        source, target = send_q.at[pair], recv_q.at[my_x, own_pair]
        if d == 0:
            pltpu.make_async_copy(source, target, q_recv.at[my_x]).start()
        else:
            pltpu.make_async_remote_copy(
                source, target, q_send, q_recv.at[my_x], device_id=at(my_y, my_x, 2 * pair + my_z % 2)
            ).start()

    pltpu.make_async_copy(send_b.at[own_pair], recv_b.at[my_y, my_z], b_recv.at[0]).start()

    @pl.loop(1, Z)
    def _(k):
        odd = k % 2
        z = (my_z + odd * ((k + 1) // 2) + (1 - odd) * (Z - k // 2)) % Z
        pltpu.make_async_remote_copy(
            send_b.at[z // 2], recv_b.at[my_y, my_z], b_send.at[0], b_recv.at[0], device_id=at(my_y, my_x, z)
        ).start()

    @pl.loop(0, GROUP)
    def _(k):
        to_group(k, lambda b, z: send_kv.at[b, z], recv_kv.at[my_i], a_send.at[0], a_recv.at[my_i])

    @pl.loop(0, GROUP)
    def _(k):
        to_group(k, lambda b, z: send_qm.at[b, z], recv_qm.at[my_i], a_send.at[1], qm_recv)

    sent(recv_q.at[my_x], q_recv.at[my_x])
    for d in (1, 3, 2):
        pltpu.make_async_remote_copy(
            recv_q.at[my_x], recv_q.at[my_x], qf_send, q_recv.at[my_x],
            device_id=at(my_y, (my_x + d) % X, my_z),
        ).start()
    sent(recv_b.at[my_y], b_recv.at[0])
    across = pltpu.make_async_remote_copy(
        recv_b.at[my_y], recv_b.at[my_y], b_send.at[1], b_recv.at[1], device_id=at(1 - my_y, my_x, my_z)
    )
    across.start()

    @pl.loop(0, GROUP)
    def _(k):
        y, dz = partner(k)
        z = (my_z + Z - dz) % Z
        i = y * Z + z
        sent(recv_kv.at[i], a_recv.at[i])
        for d in (1, 3, 2):
            pltpu.make_async_remote_copy(
                recv_kv.at[i], kvx.at[d - 1, i], f_send, f_recv.at[d - 1], device_id=at(my_y, (my_x + d) % X, my_z)
            ).start()

    def unpack(packed, out, base):
        wide = packed.astype(F32)
        out[pl.ds(base, 32)] = jnp.where(left_half, wide, 0.0).astype(BF16)
        out[pl.ds(base + 32, 32)] = jnp.where(left_half, rolled(wide), 0.0).astype(BF16)

    def rows_of(n):
        return slice(n * QB, (n + 1) * QB)

    lane_k = lanes_of((KEYS, LANES))

    def score_of(q, kv):
        return lax.dot_general(q, kv, (((1,), (1,)), ((), ())), preferred_element_type=F32)

    def softened(score, old):
        pieces = [score[:, i * LANES : (i + 1) * LANES] for i in range(KEYS // LANES)]
        top = jnp.max(functools.reduce(jnp.maximum, pieces), axis=-1, keepdims=True)
        top = jnp.broadcast_to(top, (QB, LANES))
        if old is not None:
            top = jnp.maximum(old, top)
        probs = jnp.concatenate([jnp.exp(piece - top).astype(BF16) for piece in pieces], axis=1)
        return top, probs, None if old is None else jnp.exp(old - top)

    def attend(kv, queries, old_tops, old_sums, done):
        ones_values = jnp.where(lane_k < HEAD_DIM, 1.0, kv.astype(F32)).astype(BF16)
        blocks = KEYS // QB
        score = score_of(queries(0), kv)
        for n in range(blocks):
            following = score_of(queries(n + 1), kv) if n + 1 < blocks else None
            top, probs, fade = softened(score, None if old_tops is None else old_tops(n))
            out = jnp.dot(probs, ones_values, preferred_element_type=F32)
            if fade is not None:
                out = out + fade * old_sums(n)
            done(n, top, out)
            score = following

    def main_queries(n):
        return q_main[rows_of(n)]

    def main_tops(n):
        return m_s[rows_of(n)]

    def main_sums(n):
        return acc_s[rows_of(n)]

    def keep_main(n, top, out):
        m_s[rows_of(n)] = top
        acc_s[rows_of(n)] = out

    sent(recv_qm, qm_recv)

    @pl.loop(0, GROUP)
    def _(i):
        unpack(recv_qm[i], q_main, pl.multiple_of(i * W, W))

    attend(recv_kv[...].reshape(KEYS, LANES), main_queries, None, None, keep_main)

    for d in (1, 3, 2):
        c = (my_x + d) % X
        sent(recv_q.at[c], q_recv.at[c])
    sent(recv_b.at[my_y], b_recv.at[1])

    @pl.loop(0, GROUP)
    def _(i):
        unpack(recv_q[i // 4, i % 4], q_extra, pl.multiple_of(i * W, W))

    lanes_q = lanes_of((QB, LANES))

    def extra_queries(n):
        c = (my_x + n + 1) % X
        return q_extra[pl.ds(pl.multiple_of(c * QB, QB), QB)]

    def extra_done(n, top, out):
        total = out[:, 0:1]
        hi, mid, lo = thirds(top + jnp.log(total))
        lse = jnp.where(lanes_q < 16, hi, jnp.where(lanes_q < 32, mid, lo))
        packed = jnp.where(lanes_q < HEAD_DIM, lse, out / total).astype(BF16)
        if n < X - 1:
            part_tx[n] = packed
            pltpu.make_async_remote_copy(
                part_tx.at[n], part_rx.at[my_x], p_send.at[n], p_recv, device_id=at(my_y, (my_x + n + 1) % X, my_z)
            ).start()
        else:
            part_rx[my_x] = packed

    attend(recv_b[...].reshape(KEYS, LANES), extra_queries, None, None, extra_done)

    for d in (1, 3):
        sent(kvx.at[d - 1], f_recv.at[d - 1])
        attend(kvx[d - 1].reshape(KEYS, LANES), main_queries, main_tops, main_sums, keep_main)

    def pack_rows(out, r):
        top, bottom = out[r * W : r * W + 32], out[r * W + 32 : (r + 1) * W]
        return jnp.where(left_half, rolled(top), bottom).astype(BF16)

    def home(slot, i, image, head):
        y, z = i // Z, i % Z

        @pl.when(i == my_i)
        def _():
            pltpu.make_async_copy(o_tx.at[slot], o_rx.at[image, head], o_recv).start()

        @pl.when(i != my_i)
        def _():
            pltpu.make_async_remote_copy(
                o_tx.at[slot], o_rx.at[image, head], o_send, o_recv, device_id=at(y, my_x, z)
            ).start()

    sent(part_rx.at[pl.ds(0, X - 1)], p_recv)
    parts = [part_rx[c].astype(F32) for c in range(X)]
    lses = [p[:, 0:1] + p[:, 16:17] + p[:, 32:33] for p in parts]
    peak = functools.reduce(jnp.maximum, lses)
    weights = [jnp.exp(lse - peak) for lse in lses]
    merged = sum(w * p for w, p in zip(weights, parts)) / sum(weights)
    for r in range(4):
        o_tx[GROUP + r] = pack_rows(merged, r)
    for r in range(4):
        home(GROUP + r, my_y * Z + 2 * r + my_z % 2, my_z // 4, Z + own_pair % 2)

    sent(kvx.at[1], f_recv.at[1])

    def main_done(n, top, out):
        out = out / out[:, 0:1]
        for r in range(QB // W):
            o_tx[n * (QB // W) + r] = pack_rows(out, r)
        for r in range(QB // W):
            home(n * (QB // W) + r, n * (QB // W) + r, my_y, my_z)

    attend(kvx[1].reshape(KEYS, LANES), main_queries, main_tops, main_sums, main_done)

    sent(o_rx, o_recv)
    for b in range(IMAGES):
        for j in range(HEADS // 2):
            even, odd = o_rx[b, 2 * j].astype(F32), o_rx[b, 2 * j + 1].astype(F32)
            att[b * W : b * W + 32, j * LANES : (j + 1) * LANES] = jnp.where(left_half, even, rolled(odd)).astype(BF16)
            att[b * W + 32 : (b + 1) * W, j * LANES : (j + 1) * LANES] = jnp.where(
                left_half, rolled(even), odd
            ).astype(BF16)
    loads[5].wait()
    mixed = jnp.dot(att[...], wo[...], preferred_element_type=F32)
    fresh_s[...] = (resid_s[...].astype(F32) + mixed).astype(BF16).reshape(IMAGES, W, C)
    pass_on = pltpu.make_async_remote_copy(
        fresh_s, out_hbm.at[1], h_send, h_recv, device_id={"section": (sec + 1) % 4}
    )
    pass_on.start()
    keep_copy = pltpu.make_async_copy(fresh_s, out_hbm.at[0], out_sem)
    keep_copy.start()

    below.wait_send()
    above.wait_send()
    sent(fifteen, st_send.at[0])
    sent(three, st_send.at[1])
    sent(recv_kv.at[pl.ds(0, GROUP - 1)], a_send.at[0])
    sent(recv_qm.at[pl.ds(0, GROUP - 1)], a_send.at[1])
    sent(recv_b.at[0, pl.ds(0, Z - 1)], b_send.at[0])
    across.wait_send()
    sent(send_q.at[pl.ds(0, 3)], q_send)
    sent(kvx, f_send)
    sent(recv_q.at[pl.ds(0, X - 1)], qf_send)
    for t in range(X - 1):
        sent(part_tx.at[t], p_send.at[t])
    sent(o_tx.at[pl.ds(0, GROUP + 4 - 2)], o_send)
    keep_copy.wait()
    pass_on.wait()


def body(*args):
    hbm = pl.BlockSpec(memory_space=pltpu.HBM)
    out = jax.ShapeDtypeStruct((2, IMAGES, W, C), BF16)
    dma = pltpu.SemaphoreType.DMA
    both = pl.pallas_call(
        kernel,
        out_shape=out,
        in_specs=[hbm] * 13,
        out_specs=hbm,
        scratch_shapes=[
            pltpu.SMEM((1,), jnp.int32),
            pltpu.VMEM((5, 1, C), F32),
            pltpu.VMEM((3, IMAGES, W, C), BF16),
            pltpu.VMEM((3, 3, C, C), BF16),
            pltpu.VMEM((TEMB, C), BF16),
            pltpu.VMEM((C, C), BF16),
            pltpu.VMEM((C, C), BF16),
            pltpu.VMEM((C, C), BF16),
            pltpu.VMEM((C, C), BF16),
            pltpu.VMEM((8, LANES), F32),
            pltpu.VMEM((GROUP, 8, LANES), F32),
            pltpu.VMEM((X, 8, LANES), F32),
            pltpu.VMEM((IMAGES, 3, W + 16, C), F32),
            pltpu.VMEM((IMAGES * W, 9 * C), BF16),
            pltpu.VMEM((IMAGES * W, C), BF16),
            pltpu.VMEM((IMAGES, Z, W, LANES), BF16),
            pltpu.VMEM((IMAGES, Z, W // 2, LANES), BF16),
            pltpu.VMEM((4, W, LANES), BF16),
            pltpu.VMEM((4, W // 2, LANES), BF16),
            pltpu.VMEM((GROUP, W, LANES), BF16),
            pltpu.VMEM((GROUP, W // 2, LANES), BF16),
            pltpu.VMEM((2, Z, W, LANES), BF16),
            pltpu.VMEM((X, 4, W // 2, LANES), BF16),
            pltpu.VMEM((X - 1, GROUP, W, LANES), BF16),
            pltpu.VMEM((KEYS, LANES), BF16),
            pltpu.VMEM((KEYS, LANES), BF16),
            pltpu.VMEM((KEYS, LANES), F32),
            pltpu.VMEM((KEYS, LANES), F32),
            pltpu.VMEM((X - 1, QB, LANES), BF16),
            pltpu.VMEM((X, QB, LANES), BF16),
            pltpu.VMEM((GROUP + 4, W // 2, LANES), BF16),
            pltpu.VMEM((IMAGES, HEADS, W // 2, LANES), BF16),
            pltpu.VMEM((IMAGES * W, C), BF16),
            pltpu.VMEM((IMAGES, W, C), BF16),
            dma,
            dma((6,)),
            dma((2,)),
            dma((2,)),
            dma((2,)),
            dma((2,)),
            dma((2,)),
            dma((GROUP,)),
            dma,
            dma((2,)),
            dma((2,)),
            dma,
            dma((X,)),
            dma,
            dma((X - 1,)),
            dma,
            dma((X - 1,)),
            dma,
            dma,
            dma,
            dma,
            dma,
            dma,
            dma((6,)),
        ],
        compiler_params=pltpu.CompilerParams(
            collective_id=0, has_side_effects=True, vmem_limit_bytes=63 * 1024 * 1024
        ),
    )(*args)
    whole = (1, IMAGES, 1, W, C)
    return both[0].reshape(whole), both[1].reshape(whole)


def solution(mesh):
    placed = (
        P(),
        P("section", None, "patch", None, None),
        P("section", None, None, None, None),
        P("section", None),
        P("section", None),
        P("section", None),
        P("section", None, None),
        P("section", None),
        P("section", None),
        P("section", None, None),
        P("section", None, None),
        P("section", None, None),
        P("section", None, None),
    )
    whole = P("section", None, "patch", None, None)
    return jax.shard_map(body, mesh=mesh, in_specs=placed, out_specs=(whole, whole), check_vma=False)
```

```python
import functools
import math

import jax
import jax.numpy as jnp
from jax import lax
from jax.experimental import pallas as pl
from jax.experimental.pallas import tpu as pltpu
from jax.sharding import PartitionSpec as P

GROUPS = 32
HEAD_DIM = 64
HEADS = 10
C = 640
W = 64
H = 64
IMAGES = 2
TEMB = 320
PER = C // GROUPS
LANES = 128
X = 4
Z = 8
GROUP = 16
KEYS = GROUP * W
QB = 256
F32 = jnp.float32
BF16 = jnp.bfloat16


def thirds(value):
    hi = value.astype(BF16).astype(F32)
    mid = (value - hi).astype(BF16).astype(F32)
    lo = (value - hi - mid).astype(BF16).astype(F32)
    return hi, mid, lo


def exact_dot(value, matrix):
    parts = jnp.concatenate([*thirds(value), jnp.zeros_like(value)], axis=0).astype(BF16)
    out = jnp.dot(parts, matrix, preferred_element_type=F32)
    return out[0:8] + out[8:16] + out[16:24]


def rolled(value):
    return pltpu.roll(value, HEAD_DIM, 1)


def lanes_of(shape):
    return lax.broadcasted_iota(jnp.int32, shape, 1)


def kernel(
    ts_hbm, x_hbm, ck_hbm, cb_hbm, gg_hbm, gb_hbm, tw_hbm, ng_hbm, nb_hbm, wq_hbm, wk_hbm, wv_hbm, wo_hbm,
    out_hbm,
    ts_ref, vectors, xin, wc, wt, wq, wk, wv, wo,
    stat_tx, stat_rx, stat2_rx, pad, patches, resid_s,
    send_kv, send_qm, send_b, send_q, recv_kv, recv_qm, recv_b, recv_q, kvx, q_main, q_extra,
    m_s, acc_s, part_tx, part_rx, o_tx, o_rx, att, fresh_s,
    x_sem, w_sem, st_send, st_recv, halo_send, halo_recv,
    a_send, a_recv, qm_recv, b_send, b_recv, q_send, q_recv, f_send, f_recv, qf_send, p_send, p_recv, o_send, o_recv,
    out_sem, h_send, h_recv, v_sem,
):
    me = lax.axis_index("patch")
    sec = lax.axis_index("section")
    my_y = me // (X * Z)
    my_x = (me // Z) % X
    my_z = me % Z
    my_i = my_y * Z + my_z

    def at(y, x, z):
        return {"patch": y * (X * Z) + x * Z + z}

    def sent(ref, sem):
        pltpu.make_async_copy(ref, ref, sem).wait()

    x_copy = pltpu.make_async_copy(x_hbm.at[0, :, 0], xin.at[1], x_sem)
    x_copy.start()
    loads = [
        pltpu.make_async_copy(tw_hbm.at[0], wt, w_sem.at[0]),
        pltpu.make_async_copy(ck_hbm.at[0], wc, w_sem.at[1]),
        pltpu.make_async_copy(wq_hbm.at[0], wq, w_sem.at[2]),
        pltpu.make_async_copy(wk_hbm.at[0], wk, w_sem.at[3]),
        pltpu.make_async_copy(wv_hbm.at[0], wv, w_sem.at[4]),
        pltpu.make_async_copy(wo_hbm.at[0], wo, w_sem.at[5]),
    ]
    small = [
        pltpu.make_async_copy(ref, vectors.at[n], v_sem.at[n])
        for n, ref in enumerate((cb_hbm, gg_hbm, gb_hbm, ng_hbm, nb_hbm))
    ]
    small.append(pltpu.make_async_copy(ts_hbm, ts_ref, v_sem.at[5]))
    for load in [*small, loads[0]]:
        load.start()

    barrier = pltpu.get_barrier_semaphore()

    def greet(device):
        pl.semaphore_signal(barrier, inc=1, device_id=device, device_id_type=pl.DeviceIdType.MESH)

    @pl.loop(1, GROUP)
    def _(k):
        i = (my_i + k) % GROUP
        greet(at(i // Z, my_x, i % Z))

    for k in range(1, X):
        greet(at(my_y, (my_x + k) % X, my_z))
    greet({"patch": (me + 1) % H})
    greet({"patch": (me + H - 1) % H})
    greet({"section": (sec + 1) % 4})
    greet({"section": (sec + 3) % 4})

    channel = lax.broadcasted_iota(jnp.int32, (C, LANES), 0)
    group = lax.broadcasted_iota(jnp.int32, (C, LANES), 1)
    gather = ((channel >= group * PER) & (channel < (group + 1) * PER)).astype(F32).astype(BF16)
    group_t = lax.broadcasted_iota(jnp.int32, (LANES, C), 0)
    channel_t = lax.broadcasted_iota(jnp.int32, (LANES, C), 1)
    spread = ((channel_t >= group_t * PER) & (channel_t < (group_t + 1) * PER)).astype(F32).astype(BF16)
    x_copy.wait()
    mine = xin[1].astype(F32)
    sums = [jnp.sum(mine[b], axis=0, keepdims=True) for b in range(IMAGES)]
    squares = [jnp.sum(mine[b] * mine[b], axis=0, keepdims=True) for b in range(IMAGES)]
    stacked = jnp.concatenate([*sums, *squares, jnp.zeros((4, C), F32)], axis=0)
    own_stats = exact_dot(stacked, gather)
    stat_tx[...] = own_stats
    stat_rx[my_i] = own_stats

    pl.semaphore_wait(barrier, GROUP - 1 + X - 1 + 4)

    @pl.loop(1, GROUP)
    def _(k):
        i = (my_i + k) % GROUP
        pltpu.make_async_remote_copy(
            stat_tx, stat_rx.at[my_i], st_send.at[0], st_recv.at[0], device_id=at(i // Z, my_x, i % Z)
        ).start()

    below = pltpu.make_async_remote_copy(
        xin.at[1], xin.at[0], halo_send.at[0], halo_recv.at[0], device_id={"patch": (me + 1) % H}
    )
    above = pltpu.make_async_remote_copy(
        xin.at[1], xin.at[2], halo_send.at[1], halo_recv.at[1], device_id={"patch": (me + H - 1) % H}
    )
    below.start()
    above.start()

    for load in loads[1:]:
        load.start()

    half = TEMB // 2
    place = lax.broadcasted_iota(jnp.int32, (8, TEMB), 1)
    step = jnp.where(place < half, place, place - half).astype(F32)
    for load in small:
        load.wait()
    angle = ts_ref[0].astype(F32) * jnp.exp(step * (-math.log(10000.0) / half))
    tembed = jnp.where(place < half, jnp.cos(angle), jnp.sin(angle))
    loads[0].wait()
    tproj = exact_dot(tembed * jax.nn.sigmoid(tembed), wt[...])[0:1]
    constant = tproj + vectors[0]

    fifteen = stat_rx.at[pl.ds(0, GROUP - 1)]
    sent(fifteen, st_recv.at[0])
    column_stats = jnp.sum(stat_rx[...], axis=0)
    stat2_rx[my_x] = column_stats
    for k in (1, 3, 2):
        pltpu.make_async_remote_copy(
            stat2_rx.at[my_x], stat2_rx.at[my_x], st_send.at[1], st_recv.at[1],
            device_id=at(my_y, (my_x + k) % X, my_z),
        ).start()
    three = stat2_rx.at[pl.ds(0, X - 1)]
    sent(three, st_recv.at[1])
    stats = jnp.sum(stat2_rx[...], axis=0) * (1.0 / (H * W * PER))
    mean = stats[0:2]
    rstd = lax.rsqrt(stats[2:4] - mean * mean + 1e-05)
    wide = exact_dot(jnp.concatenate([mean, rstd, jnp.zeros((4, LANES), F32)], axis=0), spread)
    scale = wide[2:4] * vectors[1]
    shift = vectors[2] - wide[0:2] * scale

    below.wait_recv()
    above.wait_recv()
    keep = [(me > 0).astype(F32), 1.0, (me < H - 1).astype(F32)]
    edge = jnp.zeros((8, C), F32)
    for b in range(IMAGES):
        for di in range(3):
            line = xin[di, b].astype(F32) * scale[b : b + 1] + shift[b : b + 1]
            line = line * jax.nn.sigmoid(line)
            if di != 1:
                line = line * keep[di]
            pad[b, di, 0:8] = edge
            pad[b, di, 72:80] = edge
            pad[b, di, 8:72] = line
            for dj in range(3):
                tap = di * 3 + dj
                patches[b * W : (b + 1) * W, tap * C : (tap + 1) * C] = pad[b, di, 7 + dj : 71 + dj].astype(BF16)
    loads[1].wait()
    conv = jnp.dot(patches[...], wc[...].reshape(9 * C, C), preferred_element_type=F32)
    resid = (xin[1].astype(F32).reshape(IMAGES * W, C) + conv + constant).astype(BF16)
    resid_s[...] = resid
    r32 = resid.astype(F32)
    centre = jnp.mean(r32, axis=-1, keepdims=True)
    off = r32 - centre
    lvar = jnp.mean(off * off, axis=-1, keepdims=True)
    normed = (off * lax.rsqrt(lvar + 1e-05) * vectors[3] + vectors[4]).astype(BF16)

    left = lanes_of((W, LANES)) < HEAD_DIM
    left_half = lanes_of((W // 2, LANES)) < HEAD_DIM
    for load in loads[2:5]:
        load.wait()
    queries = jnp.dot(normed, wq[...], preferred_element_type=F32) * (HEAD_DIM**-0.5)
    keys = jnp.dot(normed, wk[...], preferred_element_type=F32)
    values = jnp.dot(normed, wv[...], preferred_element_type=F32)
    for b in range(IMAGES):
        rows = slice(b * W, (b + 1) * W)
        for j in range(HEADS // 2):
            lanes = slice(j * LANES, (j + 1) * LANES)
            k_pair, v_pair, q_pair = keys[rows, lanes], values[rows, lanes], queries[rows, lanes]
            top, bottom = q_pair[: W // 2], q_pair[W // 2 :]
            kv = (jnp.where(left, k_pair, rolled(v_pair)), jnp.where(left, rolled(k_pair), v_pair))
            qq = (jnp.where(left_half, top, rolled(bottom)), jnp.where(left_half, rolled(top), bottom))
            for e in range(2):
                head = 2 * j + e
                if head < Z:
                    send_qm[b, head] = qq[e].astype(BF16)
                    send_kv[b, head] = kv[e].astype(BF16)
                else:
                    send_q[b * 2 + head - Z] = qq[e].astype(BF16)
                    send_b[b * 2 + head - Z] = kv[e].astype(BF16)

    def partner(k):
        m = k // 2
        odd = m % 2
        dz = odd * ((m + 1) // 2) + (1 - odd) * ((Z - m // 2) % Z)
        return (my_y + k % 2) % 2, dz

    def to_group(k, source, target, send_sem, recv_sem):
        b, dz = partner(k)
        z = (my_z + dz) % Z

        @pl.when(k == 0)
        def _():
            pltpu.make_async_copy(source(b, z), target, recv_sem).start()

        @pl.when(k > 0)
        def _():
            pltpu.make_async_remote_copy(
                source(b, z), target, send_sem, recv_sem, device_id=at(b, my_x, z)
            ).start()

    own_pair = my_z // 2
    for d in range(4):
        pair = (own_pair + d) % 4
        source, target = send_q.at[pair], recv_q.at[my_x, own_pair]
        if d == 0:
            pltpu.make_async_copy(source, target, q_recv.at[my_x]).start()
        else:
            pltpu.make_async_remote_copy(
                source, target, q_send, q_recv.at[my_x], device_id=at(my_y, my_x, 2 * pair + my_z % 2)
            ).start()

    pltpu.make_async_copy(send_b.at[own_pair], recv_b.at[my_y, my_z], b_recv.at[0]).start()

    @pl.loop(1, Z)
    def _(k):
        odd = k % 2
        z = (my_z + odd * ((k + 1) // 2) + (1 - odd) * (Z - k // 2)) % Z
        pltpu.make_async_remote_copy(
            send_b.at[z // 2], recv_b.at[my_y, my_z], b_send.at[0], b_recv.at[0], device_id=at(my_y, my_x, z)
        ).start()

    @pl.loop(0, GROUP)
    def _(k):
        to_group(k, lambda b, z: send_kv.at[b, z], recv_kv.at[my_i], a_send.at[0], a_recv.at[my_i])

    @pl.loop(0, GROUP)
    def _(k):
        to_group(k, lambda b, z: send_qm.at[b, z], recv_qm.at[my_i], a_send.at[1], qm_recv)

    sent(recv_q.at[my_x], q_recv.at[my_x])
    for d in (1, 3, 2):
        pltpu.make_async_remote_copy(
            recv_q.at[my_x], recv_q.at[my_x], qf_send, q_recv.at[my_x],
            device_id=at(my_y, (my_x + d) % X, my_z),
        ).start()
    sent(recv_b.at[my_y], b_recv.at[0])
    across = pltpu.make_async_remote_copy(
        recv_b.at[my_y], recv_b.at[my_y], b_send.at[1], b_recv.at[1], device_id=at(1 - my_y, my_x, my_z)
    )
    across.start()

    @pl.loop(0, GROUP)
    def _(k):
        y, dz = partner(k)
        z = (my_z + Z - dz) % Z
        i = y * Z + z
        sent(recv_kv.at[i], a_recv.at[i])
        for d in (1, 3, 2):
            pltpu.make_async_remote_copy(
                recv_kv.at[i], kvx.at[d - 1, i], f_send, f_recv.at[d - 1], device_id=at(my_y, (my_x + d) % X, my_z)
            ).start()

    def unpack(packed, out, base):
        wide = packed.astype(F32)
        out[pl.ds(base, 32)] = jnp.where(left_half, wide, 0.0).astype(BF16)
        out[pl.ds(base + 32, 32)] = jnp.where(left_half, rolled(wide), 0.0).astype(BF16)

    def rows_of(n):
        return slice(n * QB, (n + 1) * QB)

    lane_k = lanes_of((KEYS, LANES))

    def score_of(q, kv):
        return lax.dot_general(q, kv, (((1,), (1,)), ((), ())), preferred_element_type=F32)

    def softened(score, old):
        pieces = [score[:, i * LANES : (i + 1) * LANES] for i in range(KEYS // LANES)]
        top = jnp.max(functools.reduce(jnp.maximum, pieces), axis=-1, keepdims=True)
        top = jnp.broadcast_to(top, (QB, LANES))
        if old is not None:
            top = jnp.maximum(old, top)
        probs = jnp.concatenate([jnp.exp(piece - top).astype(BF16) for piece in pieces], axis=1)
        return top, probs, None if old is None else jnp.exp(old - top)

    def attend(kv, queries, old_tops, old_sums, done):
        ones_values = jnp.where(lane_k < HEAD_DIM, 1.0, kv.astype(F32)).astype(BF16)
        blocks = KEYS // QB
        score = score_of(queries(0), kv)
        for n in range(blocks):
            following = score_of(queries(n + 1), kv) if n + 1 < blocks else None
            top, probs, fade = softened(score, None if old_tops is None else old_tops(n))
            out = jnp.dot(probs, ones_values, preferred_element_type=F32)
            if fade is not None:
                out = out + fade * old_sums(n)
            done(n, top, out)
            score = following

    def main_queries(n):
        return q_main[rows_of(n)]

    def main_tops(n):
        return m_s[rows_of(n)]

    def main_sums(n):
        return acc_s[rows_of(n)]

    def keep_main(n, top, out):
        m_s[rows_of(n)] = top
        acc_s[rows_of(n)] = out

    for d in (1, 3, 2):
        c = (my_x + d) % X
        sent(recv_q.at[c], q_recv.at[c])
    sent(recv_b.at[my_y], b_recv.at[1])

    @pl.loop(0, GROUP)
    def _(i):
        unpack(recv_q[i // 4, i % 4], q_extra, pl.multiple_of(i * W, W))

    lanes_q = lanes_of((QB, LANES))

    def extra_queries(n):
        c = (my_x + n + 1) % X
        return q_extra[pl.ds(pl.multiple_of(c * QB, QB), QB)]

    def extra_done(n, top, out):
        total = out[:, 0:1]
        hi, mid, lo = thirds(top + jnp.log(total))
        lse = jnp.where(lanes_q < 16, hi, jnp.where(lanes_q < 32, mid, lo))
        packed = jnp.where(lanes_q < HEAD_DIM, lse, out / total).astype(BF16)
        if n < X - 1:
            part_tx[n] = packed
            pltpu.make_async_remote_copy(
                part_tx.at[n], part_rx.at[my_x], p_send.at[n], p_recv, device_id=at(my_y, (my_x + n + 1) % X, my_z)
            ).start()
        else:
            part_rx[my_x] = packed

    attend(recv_b[...].reshape(KEYS, LANES), extra_queries, None, None, extra_done)

    sent(recv_qm, qm_recv)

    @pl.loop(0, GROUP)
    def _(i):
        unpack(recv_qm[i], q_main, pl.multiple_of(i * W, W))

    attend(recv_kv[...].reshape(KEYS, LANES), main_queries, None, None, keep_main)
    for d in (1, 3):
        sent(kvx.at[d - 1], f_recv.at[d - 1])
        attend(kvx[d - 1].reshape(KEYS, LANES), main_queries, main_tops, main_sums, keep_main)

    def pack_rows(out, r):
        top, bottom = out[r * W : r * W + 32], out[r * W + 32 : (r + 1) * W]
        return jnp.where(left_half, rolled(top), bottom).astype(BF16)

    def home(slot, i, image, head):
        y, z = i // Z, i % Z

        @pl.when(i == my_i)
        def _():
            pltpu.make_async_copy(o_tx.at[slot], o_rx.at[image, head], o_recv).start()

        @pl.when(i != my_i)
        def _():
            pltpu.make_async_remote_copy(
                o_tx.at[slot], o_rx.at[image, head], o_send, o_recv, device_id=at(y, my_x, z)
            ).start()

    sent(kvx.at[1], f_recv.at[1])

    def main_done(n, top, out):
        out = out / out[:, 0:1]
        for r in range(QB // W):
            o_tx[n * (QB // W) + r] = pack_rows(out, r)
        for r in range(QB // W):
            home(n * (QB // W) + r, n * (QB // W) + r, my_y, my_z)

    attend(kvx[1].reshape(KEYS, LANES), main_queries, main_tops, main_sums, main_done)

    sent(part_rx.at[pl.ds(0, X - 1)], p_recv)
    parts = [part_rx[c].astype(F32) for c in range(X)]
    lses = [p[:, 0:1] + p[:, 16:17] + p[:, 32:33] for p in parts]
    peak = functools.reduce(jnp.maximum, lses)
    weights = [jnp.exp(lse - peak) for lse in lses]
    merged = sum(w * p for w, p in zip(weights, parts)) / sum(weights)
    for r in range(4):
        o_tx[GROUP + r] = pack_rows(merged, r)
    for r in range(4):
        home(GROUP + r, my_y * Z + 2 * r + my_z % 2, my_z // 4, Z + own_pair % 2)

    sent(o_rx, o_recv)
    for b in range(IMAGES):
        for j in range(HEADS // 2):
            even, odd = o_rx[b, 2 * j].astype(F32), o_rx[b, 2 * j + 1].astype(F32)
            att[b * W : b * W + 32, j * LANES : (j + 1) * LANES] = jnp.where(left_half, even, rolled(odd)).astype(BF16)
            att[b * W + 32 : (b + 1) * W, j * LANES : (j + 1) * LANES] = jnp.where(
                left_half, rolled(even), odd
            ).astype(BF16)
    loads[5].wait()
    mixed = jnp.dot(att[...], wo[...], preferred_element_type=F32)
    fresh_s[...] = (resid_s[...].astype(F32) + mixed).astype(BF16).reshape(IMAGES, W, C)
    pass_on = pltpu.make_async_remote_copy(
        fresh_s, out_hbm.at[1], h_send, h_recv, device_id={"section": (sec + 1) % 4}
    )
    pass_on.start()
    keep_copy = pltpu.make_async_copy(fresh_s, out_hbm.at[0], out_sem)
    keep_copy.start()

    below.wait_send()
    above.wait_send()
    sent(fifteen, st_send.at[0])
    sent(three, st_send.at[1])
    sent(recv_kv.at[pl.ds(0, GROUP - 1)], a_send.at[0])
    sent(recv_qm.at[pl.ds(0, GROUP - 1)], a_send.at[1])
    sent(recv_b.at[0, pl.ds(0, Z - 1)], b_send.at[0])
    across.wait_send()
    sent(send_q.at[pl.ds(0, 3)], q_send)
    sent(kvx, f_send)
    sent(recv_q.at[pl.ds(0, X - 1)], qf_send)
    for t in range(X - 1):
        sent(part_tx.at[t], p_send.at[t])
    sent(o_tx.at[pl.ds(0, GROUP + 4 - 2)], o_send)
    keep_copy.wait()
    pass_on.wait()


def body(*args):
    hbm = pl.BlockSpec(memory_space=pltpu.HBM)
    out = jax.ShapeDtypeStruct((2, IMAGES, W, C), BF16)
    dma = pltpu.SemaphoreType.DMA
    both = pl.pallas_call(
        kernel,
        out_shape=out,
        in_specs=[hbm] * 13,
        out_specs=hbm,
        scratch_shapes=[
            pltpu.SMEM((1,), jnp.int32),
            pltpu.VMEM((5, 1, C), F32),
            pltpu.VMEM((3, IMAGES, W, C), BF16),
            pltpu.VMEM((3, 3, C, C), BF16),
            pltpu.VMEM((TEMB, C), BF16),
            pltpu.VMEM((C, C), BF16),
            pltpu.VMEM((C, C), BF16),
            pltpu.VMEM((C, C), BF16),
            pltpu.VMEM((C, C), BF16),
            pltpu.VMEM((8, LANES), F32),
            pltpu.VMEM((GROUP, 8, LANES), F32),
            pltpu.VMEM((X, 8, LANES), F32),
            pltpu.VMEM((IMAGES, 3, W + 16, C), F32),
            pltpu.VMEM((IMAGES * W, 9 * C), BF16),
            pltpu.VMEM((IMAGES * W, C), BF16),
            pltpu.VMEM((IMAGES, Z, W, LANES), BF16),
            pltpu.VMEM((IMAGES, Z, W // 2, LANES), BF16),
            pltpu.VMEM((4, W, LANES), BF16),
            pltpu.VMEM((4, W // 2, LANES), BF16),
            pltpu.VMEM((GROUP, W, LANES), BF16),
            pltpu.VMEM((GROUP, W // 2, LANES), BF16),
            pltpu.VMEM((2, Z, W, LANES), BF16),
            pltpu.VMEM((X, 4, W // 2, LANES), BF16),
            pltpu.VMEM((X - 1, GROUP, W, LANES), BF16),
            pltpu.VMEM((KEYS, LANES), BF16),
            pltpu.VMEM((KEYS, LANES), BF16),
            pltpu.VMEM((KEYS, LANES), F32),
            pltpu.VMEM((KEYS, LANES), F32),
            pltpu.VMEM((X - 1, QB, LANES), BF16),
            pltpu.VMEM((X, QB, LANES), BF16),
            pltpu.VMEM((GROUP + 4, W // 2, LANES), BF16),
            pltpu.VMEM((IMAGES, HEADS, W // 2, LANES), BF16),
            pltpu.VMEM((IMAGES * W, C), BF16),
            pltpu.VMEM((IMAGES, W, C), BF16),
            dma,
            dma((6,)),
            dma((2,)),
            dma((2,)),
            dma((2,)),
            dma((2,)),
            dma((2,)),
            dma((GROUP,)),
            dma,
            dma((2,)),
            dma((2,)),
            dma,
            dma((X,)),
            dma,
            dma((X - 1,)),
            dma,
            dma((X - 1,)),
            dma,
            dma,
            dma,
            dma,
            dma,
            dma,
            dma((6,)),
        ],
        compiler_params=pltpu.CompilerParams(
            collective_id=0, has_side_effects=True, vmem_limit_bytes=63 * 1024 * 1024
        ),
    )(*args)
    whole = (1, IMAGES, 1, W, C)
    return both[0].reshape(whole), both[1].reshape(whole)


def solution(mesh):
    placed = (
        P(),
        P("section", None, "patch", None, None),
        P("section", None, None, None, None),
        P("section", None),
        P("section", None),
        P("section", None),
        P("section", None, None),
        P("section", None),
        P("section", None),
        P("section", None, None),
        P("section", None, None),
        P("section", None, None),
        P("section", None, None),
    )
    whole = P("section", None, "patch", None, None)
    return jax.shard_map(body, mesh=mesh, in_specs=placed, out_specs=(whole, whole), check_vma=False)
```
